32 devices in a mesh: phase: 4 (over x, core), seq: 8 (over z, y).
Axes of the slice: x: 2, y: 2, z: 4, core: 2. Of those that a mesh axis runs over, the one named last changes fastest.
Arguments:
- frames: bfloat16 [4, 1280, 1024], P('phase', 'seq'), may hold values from -6 to 6
- lengths: int32 [4, 8], P('phase'), may hold values from 1 to 640, 1280 in all within a row
- w_query: bfloat16 [4, 1024, 1024], P('phase', None, 'seq'), may hold values from -1 to 1
- w_key: bfloat16 [4, 1024, 1024], P('phase', None, 'seq'), may hold values from -1 to 1
- w_value: bfloat16 [4, 1024, 1024], P('phase', None, 'seq'), may hold values from -0.1875 to 0.1875
- w_output: bfloat16 [4, 1024, 1024], P('phase', None, 'seq'), may hold values from -0.1875 to 0.1875
- conv_in: bfloat16 [4, 1024, 2048], P('phase', None, 'seq'), may hold values from -0.1875 to 0.1875
- conv_taps: bfloat16 [4, 31, 1024], P('phase'), may hold values from -1 to 1
- conv_out: bfloat16 [4, 1024, 1024], P('phase', None, 'seq'), may hold values from -0.1875 to 0.1875
Outputs:
- handed: bfloat16 [4, 1280, 1024], P('phase', 'seq')
The draws below stay inside these ranges and needn't reach their ends.
Inputs may be any that keep to these rules, and one draw needn't show every extreme that they name: Each phase's lengths sum to 1280 and the largest equals 640.
All inputs are finite; a program needn't handle non-finite values.
Results may differ from the reference program's by a relative error of at most 0.0085.
Values may be sent and summed in bfloat16 or wider, within the bound.
A program may use at most 64 MiB of HBM per device.

```python
import math
import jax
import jax.numpy as jnp
import numpy as np
from jax import lax

D = 1024
HEADS = 16
KERNEL = 31
UTTS = 8
FRAMES = 1280
N_PHASE = 4


def projection(key, salt):
    shared = jax.random.normal(jax.random.fold_in(key, 101), (N_PHASE, D, D), jnp.float32)
    own = jax.random.normal(jax.random.fold_in(key, salt), (N_PHASE, D, D), jnp.float32)
    mixed = 0.6 * shared + 0.8 * own
    return jnp.clip(mixed / math.sqrt(D), -1.0, 1.0).astype(jnp.bfloat16)


def draw_w_query(key, part):
    return projection(key, 102)


def draw_w_key(key, part):
    return projection(key, 103)


def steps_of(stream_key, dims, shards, least, top_value):
    def one(dim, blocks):
        steps = jax.random.uniform(jax.random.fold_in(jax.random.fold_in(stream_key, 6), dim), (blocks,), jnp.float32, least / len(shards), top_value / len(shards))
        return jnp.repeat(jnp.exp(steps), dims[dim] // blocks).reshape((-1,) + (1,) * (len(dims) - dim - 1))

    loudness = one(*shards[0])
    for cut in shards[1:]:
        loudness = loudness * one(*cut)
    return loudness


def length_profile(amount, total, most, slope):
    loads = [(1 << 20) // math.isqrt(grade ** slope) + 1 for grade in range(2, amount + 1)]
    rest, holding = total - most - (amount - 1), [1] * (amount - 1)
    while rest > 0:
        candidates = [i for i in range(amount - 1) if holding[i] < most]
        mass, left = sum([loads[i] for i in candidates]), rest
        for i in candidates:
            more = min(most - holding[i], max(1, left * loads[i] // mass), rest)
            holding[i] = holding[i] + more
            rest = rest - more
    return np.array([most] + holding)


def uneven_parts(key, number_of, total, limit, skew):
    if number_of == 2:
        one = jax.random.randint(key, (), max(1, total - limit), min(limit, total - 1) + 1)
        return jnp.stack([one, total - one])
    sizes = jnp.asarray(length_profile(number_of, total, limit, skew), jnp.int32)
    twos = (number_of - 1) // 2
    giver, sink = sizes[1:1 + 2 * twos:2], sizes[2:2 + 2 * twos:2]
    slack = jnp.minimum(giver - 1, limit - sink)
    moved = jax.random.randint(jax.random.fold_in(key, 1), (twos,), 0, 1 << 20) % (slack + 1)
    sizes = sizes.at[1:1 + 2 * twos:2].set(giver - moved).at[2:2 + 2 * twos:2].set(sink + moved)
    return sizes[jax.random.permutation(jax.random.fold_in(key, 2), number_of)]


def scatter_about(stream_key, extent, deviation, most, split=(), held_as=jnp.bfloat16):
    gain = steps_of(stream_key, extent, split, -0.22, 0.18) if split else 1.0
    values = jax.random.normal(stream_key, extent, jnp.float32) * deviation * gain
    return jnp.minimum(jnp.maximum(values, -most), most).astype(held_as)


def setup_inputs(seed: int = 0) -> dict:
    keys = jax.random.split(jax.random.key(seed), 10)
    return {
        "frames": scatter_about(keys[0], (N_PHASE, FRAMES, D), 1.0, 6.0, ((0, 4), (1, 8))),
        "lengths": jax.vmap(lambda own: uneven_parts(own, UTTS, FRAMES, FRAMES // 2, 2))(jax.random.split(keys[1], N_PHASE)).reshape((N_PHASE, UTTS)).astype(jnp.int32),
        "w_query": draw_w_query(jax.random.fold_in(keys[9], 71), 0),
        "w_key": draw_w_key(jax.random.fold_in(keys[9], 71), 0),
        "w_value": scatter_about(keys[4], (N_PHASE, D, D), D ** -0.5, 0.1875, ((0, 4), (2, 8))),
        "w_output": scatter_about(keys[5], (N_PHASE, D, D), D ** -0.5, 0.1875, ((0, 4), (2, 8))),
        "conv_in": scatter_about(keys[6], (N_PHASE, D, 2 * D), D ** -0.5, 0.1875, ((0, 4), (2, 8))),
        "conv_taps": scatter_about(keys[7], (N_PHASE, KERNEL, D), KERNEL ** -0.5, 1.0, ((0, 4),)),
        "conv_out": scatter_about(keys[8], (N_PHASE, D, D), D ** -0.5, 0.1875, ((0, 4), (2, 8))),
    }


def layer_norm(values):
    centre = values - lax.optimization_barrier(jnp.mean(values, axis=-1, keepdims=True))
    spread = lax.optimization_barrier(jnp.mean(centre * centre, axis=-1, keepdims=True))
    return centre * lax.rsqrt(spread + 1e-05)

def segment_ids(positions, lengths):
    bounds = jnp.cumsum(lengths).astype(jnp.int32)
    return lax.optimization_barrier(jnp.sum((positions[:, None] >= bounds[None, :]).astype(jnp.int32), axis=1)).astype(jnp.int32)

def conformer_block(hidden, lengths, w_query, w_key, w_value, w_output, conv_in, conv_taps, conv_out):
    total_rows = hidden.shape[0]
    width = hidden.shape[1]
    head_size = width // HEADS
    scale = 1.0 / math.sqrt(head_size)
    normed = layer_norm(hidden.astype(jnp.float32)).astype(jnp.bfloat16)
    query = jnp.dot(normed, w_query, preferred_element_type=jnp.float32).astype(jnp.bfloat16)
    key_proj = jnp.dot(normed, w_key, preferred_element_type=jnp.float32).astype(jnp.bfloat16)
    value_proj = jnp.dot(normed, w_value, preferred_element_type=jnp.float32).astype(jnp.bfloat16)
    segment = segment_ids(jnp.arange(total_rows, dtype=jnp.int32), lengths)
    same_utt = segment[:, None] == segment[None, :]

    def one_head(operands):
        head_query, head_key, head_value = operands
        scores = jnp.dot(head_query, head_key.T, preferred_element_type=jnp.float32) * scale
        scores = jnp.where(same_utt, scores, -1e+30)
        peak = lax.optimization_barrier(jnp.max(scores, axis=1, keepdims=True))
        expw = jnp.where(same_utt, jnp.exp(scores - peak), 0.0)
        total_weight = lax.optimization_barrier(jnp.sum(expw, axis=1, keepdims=True))
        mixed = jnp.dot(expw.astype(jnp.bfloat16), head_value, preferred_element_type=jnp.float32) / total_weight
        return mixed.astype(jnp.bfloat16)

    def split_heads(matrix):
        return matrix.reshape(total_rows, HEADS, head_size).transpose(1, 0, 2)
    attended = lax.map(one_head, (split_heads(query), split_heads(key_proj), split_heads(value_proj)))
    attended = attended.transpose(1, 0, 2).reshape(total_rows, width)
    after_attn = hidden.astype(jnp.float32) + jnp.dot(attended, w_output, preferred_element_type=jnp.float32)
    conv_normed = layer_norm(after_attn).astype(jnp.bfloat16)
    gates = jnp.dot(conv_normed, conv_in, preferred_element_type=jnp.float32)
    glu = (gates[:, :width] * jax.nn.sigmoid(gates[:, width:])).astype(jnp.bfloat16)
    reach = KERNEL // 2
    padded = jnp.pad(glu, ((reach, reach), (0, 0)))
    padded_seg = jnp.pad(segment, (reach, reach), constant_values=-1)
    depthwise = jnp.zeros((total_rows, width), jnp.float32)
    for offset in range(KERNEL):
        keep = padded_seg[offset:offset + total_rows] == segment
        term = padded[offset:offset + total_rows].astype(jnp.float32) * conv_taps[offset].astype(jnp.float32)
        depthwise = depthwise + jnp.where(keep[:, None], term, 0.0)
    conv_act = layer_norm(depthwise)
    conv_act = (conv_act * jax.nn.sigmoid(conv_act)).astype(jnp.bfloat16)
    result = after_attn + jnp.dot(conv_act, conv_out, preferred_element_type=jnp.float32)
    return result.astype(jnp.bfloat16)

def reference(frames, lengths, w_query, w_key, w_value, w_output, conv_in, conv_taps, conv_out):
    outputs = []
    for phase_idx in range(N_PHASE):
        outputs.append(conformer_block(frames[phase_idx], lengths[phase_idx], w_query[phase_idx], w_key[phase_idx], w_value[phase_idx], w_output[phase_idx], conv_in[phase_idx], conv_taps[phase_idx], conv_out[phase_idx]))
    stacked = jnp.stack(outputs)
    return jnp.roll(stacked, 1, axis=0)
```

```python
import functools
import math

import jax
import jax.numpy as jnp
from jax import lax
from jax.experimental import pallas as pl
from jax.experimental.pallas import tpu as pltpu
from jax.sharding import PartitionSpec as P

HEADS = 16
KERNEL = 31
MESH = pl.DeviceIdType.MESH


def padded_2(block, sides, width):
    for axis, dim in sides:
        count = lax.axis_size(axis)
        forward = [(i, i + 1) for i in range(count - 1)]
        backward = [(target, source) for source, target in forward]
        low = lax.ppermute(
            lax.slice_in_dim(block, block.shape[dim] - width, None, axis=dim), axis, forward
        )
        high = lax.ppermute(lax.slice_in_dim(block, 0, width, axis=dim), axis, backward)
        block = jnp.concatenate([low, block, high], axis=dim)
    return block


def passed_along(block, axis, distance):
    devices = range(lax.axis_size(axis))
    route = [((i - distance) % len(devices), i) for i in devices]
    return lax.ppermute(block, axis, route)


def layer_norm(values):
    centre = values - jnp.mean(values, axis=-1, keepdims=True)
    spread = jnp.mean(centre * centre, axis=-1, keepdims=True)
    return centre * lax.rsqrt(spread + 1e-05)


def segment_ids(positions, lengths):
    order = jnp.arange(lengths.shape[0], dtype=jnp.int32)
    bounds = jnp.sum(jnp.where(order[None, :] <= order[:, None], lengths[None, :], 0), axis=1)
    return jnp.sum((positions[:, None] >= bounds[None, :]).astype(jnp.int32), axis=1)


def ring_index(place, shards):
    place = lax.rem(place + shards, shards)
    late = lax.div(place, shards // 2)
    return (1 - late) * (2 * place) + late * (2 * (shards - 1 - place) + 1)


def segment_of(positions, bounds):
    segment = jnp.zeros(positions.shape, jnp.int32)
    for bound in bounds:
        segment = segment + (positions >= bound).astype(jnp.int32)
    return segment


def block_kernel(
    shards,
    head_size,
    lengths_ref,
    frames_ref,
    taps_ref,
    query_ref,
    key_ref,
    value_ref,
    w_a_ref,
    w_b_ref,
    w_c_ref,
    handed_ref,
    hidden,
    qkv,
    full_a_ref,
    half_b_ref,
    full_c_ref,
    attended_ref,
    after,
    conv_rows,
    near,
    taps,
    padded,
    depthwise,
    deep_out,
    deep_in,
    leaving,
    normed,
    query,
    keys,
    values,
    outbox,
    send_sem,
    recv_sem,
    own_sem,
    out_send,
    out_recv,
    in_sem,
    b_send,
    b_recv,
    rows_send,
    rows_recv,
    edge_send,
    edge_recv,
    deep_send,
    deep_recv,
    leave_send,
    leave_recv,
):
    rows = frames_ref.shape[0]
    depth = frames_ref.shape[1]
    width = query_ref.shape[1]
    loads_in = [pltpu.make_async_copy(frames_ref, hidden, in_sem.at[3])]
    for i, ref in enumerate((query_ref, key_ref, value_ref)):
        loads_in.append(
            pltpu.make_async_copy(ref, qkv.at[:, pl.ds(i * width, width)], in_sem.at[i])
        )
    for copy in loads_in:
        copy.start()
    steps = shards // 2
    me = lax.axis_index("seq")
    odd = lax.rem(me, 2)
    place = (1 - odd) * lax.div(me, 2) + odd * (shards - 1 - lax.div(me, 2))
    right, left = ring_index(place + 1, shards), ring_index(place - 1, shards)
    half = lax.rem(lax.div(me, 2), 2)
    upper = lax.div(me, 4)

    def partner_of(owner):
        return owner + 2 - 4 * lax.rem(lax.div(owner, 2), 2)

    beside = me + 1 - 2 * odd
    across = me + 4 - 8 * upper
    partner = partner_of(me)

    barrier = pltpu.get_barrier_semaphore()
    for away in range(1, shards):
        peer = lax.rem(me + away, shards)
        pl.semaphore_signal(barrier, inc=1, device_id={"seq": peer}, device_id_type=MESH)
    phase = lax.axis_index("phase")
    phases = lax.axis_size("phase")
    phase_next = lax.rem(phase + 1, phases)
    phase_back = lax.rem(phase + phases - 1, phases)
    for peer in (phase_next, phase_back):
        pl.semaphore_signal(barrier, inc=1, device_id={"phase": peer}, device_id_type=MESH)

    loads_in[0].wait()
    own_rows = pl.ds(pl.multiple_of(me * rows, rows), rows)
    normed[own_rows, :] = layer_norm(hidden[...].astype(jnp.float32)).astype(jnp.bfloat16)
    pl.semaphore_wait(barrier, shards + 1)

    rings = {1: (w_a_ref, full_a_ref), 2: (w_c_ref, full_c_ref)}

    def hop(load, step, way, piece):
        owner = ring_index(place - step if way == 0 else place + step, shards)
        if load == 0:
            size = rows // 2
            first = pl.multiple_of(owner * rows + piece * size, 16)
            source = target = normed.at[pl.ds(first, size), :]
        else:
            own, full = rings[load]
            size = own.shape[0] // 2
            target = full.at[owner, pl.ds(piece * size, size), :]
            source = own.at[pl.ds(piece * size, size), :] if step == 0 else target
        at = (load * steps + step) * 2 + way
        return pltpu.make_async_remote_copy(
            src_ref=source,
            dst_ref=target,
            send_sem=send_sem.at[at, piece],
            recv_sem=recv_sem.at[at, piece],
            device_id={"seq": right if way == 0 else left},
            device_id_type=MESH,
        )

    def hops(step):
        pairs = [(way, piece) for piece in range(2) for way in range(2)]
        return [(way, piece) for way, piece in pairs if step < steps - 1 or way == piece]

    def send(load):
        for way, piece in hops(0):
            hop(load, 0, way, piece).start()

    def forward(load, step):
        onward = hops(step + 1) if step < steps - 1 else ()
        for way, piece in hops(step):
            hop(load, step, way, piece).wait_recv()
            if (way, piece) in onward:
                hop(load, step + 1, way, piece).start()

    def project(owner):
        at = pl.ds(pl.multiple_of(owner * rows, rows), rows)
        block = normed[at, :]
        both = jnp.dot(block, qkv[...], preferred_element_type=jnp.float32).astype(jnp.bfloat16)
        query[at, :] = both[:, :width] * jnp.bfloat16(1.0 / math.sqrt(head_size))
        keys[at, :] = both[:, width : 2 * width]
        values[at, :] = both[:, 2 * width :]

    def b_slot(owner):
        return lax.div(owner, 4) * 2 + lax.rem(owner, 2)

    def b_copy(kind, piece):
        size = w_b_ref.shape[0] // 2
        at = pl.ds(piece * size, size)
        slot = b_slot(across if kind == 2 else me)
        target = half_b_ref.at[slot, at, :]
        return pltpu.make_async_remote_copy(
            src_ref=target if kind == 2 else w_b_ref.at[at, :],
            dst_ref=target,
            send_sem=b_send.at[kind, piece],
            recv_sem=b_recv.at[kind, piece],
            device_id={"seq": across if kind == 0 else beside},
            device_id_type=MESH,
        )

    send(0)
    kept = [
        pltpu.make_async_copy(w_a_ref, full_a_ref.at[me], own_sem.at[0]),
        pltpu.make_async_copy(w_b_ref, half_b_ref.at[b_slot(me)], own_sem.at[1]),
        pltpu.make_async_copy(w_c_ref, full_c_ref.at[me], own_sem.at[2]),
    ]
    for copy in kept:
        copy.start()

    bounds = [lengths_ref[0]]
    for utt in range(1, lengths_ref.shape[0]):
        bounds.append(bounds[-1] + lengths_ref[utt])
    seg_col = segment_of(lax.broadcasted_iota(jnp.int32, (1, rows * shards), 1), bounds)
    margin = (near.shape[1] - rows) // 2
    for slot, owner in enumerate((me, partner)):
        positions = lax.broadcasted_iota(jnp.int32, near.shape[1:], 0) + (owner * rows - margin)
        near[slot] = jnp.where(positions >= 0, segment_of(positions, bounds), -1)
    taps[...] = taps_ref[...].astype(jnp.float32)

    for copy in loads_in[1:]:
        copy.wait()
    project(me)
    for step in range(steps):
        forward(0, step)
        if step == steps - 2:
            send(1)
        project(ring_index(place - 1 - step, shards))
        if step < steps - 1:
            project(ring_index(place + 1 + step, shards))

    lane = lax.broadcasted_iota(jnp.int32, (rows, width), 1)
    my_columns = pl.ds(pl.multiple_of(me * width, 128), width)

    def attend(owner):
        at = pl.ds(pl.multiple_of(owner * rows, rows), rows)
        block = query[at, :]
        positions = lax.broadcasted_iota(jnp.int32, (rows, 1), 0) + owner * rows
        allowed = segment_of(positions, bounds) == seg_col
        result = jnp.zeros((rows, width), jnp.float32)
        for head in range(width // head_size):
            mine = (lane >= head * head_size) & (lane < (head + 1) * head_size)
            scores = lax.dot_general(
                jnp.where(mine, block, jnp.bfloat16(0)),
                keys[...],
                (((1,), (1,)), ((), ())),
                preferred_element_type=jnp.float32,
            )
            scores = jnp.where(allowed, scores, -1e30)
            peak = jnp.max(scores, axis=1, keepdims=True)
            expw = jnp.exp(scores - peak)
            total = jnp.sum(expw, axis=1, keepdims=True)
            mixed = jnp.dot(
                expw.astype(jnp.bfloat16), values[...], preferred_element_type=jnp.float32
            )
            result = jnp.where(mine, mixed / total, result)
        return result.astype(jnp.bfloat16)

    def out_copy(away):
        peer = lax.rem(me + away, shards)
        return pltpu.make_async_remote_copy(
            src_ref=outbox.at[away - 1],
            dst_ref=attended_ref.at[:, my_columns],
            send_sem=out_send.at[away - 1],
            recv_sem=out_recv.at[away - 1],
            device_id={"seq": peer},
            device_id_type=MESH,
        )

    for away in range(1, shards + 1):
        if away < shards:
            outbox[away - 1] = attend(lax.rem(me + away, shards))
            out_copy(away).start()
        else:
            attended_ref[:, my_columns] = attend(me)
        if away == 4:
            forward(1, 0)
    forward(1, 1)
    for piece in range(2):
        b_copy(0, piece).start()
    for piece in range(2):
        b_copy(1, piece).start()
    forward(1, 2)
    for away in range(1, shards):
        out_copy(away).wait_recv()
    kept[0].wait()
    forward(1, 3)
    tile = 2 * width

    def joined(full, pair):
        return jnp.concatenate([full[2 * pair], full[2 * pair + 1]], axis=1)

    for at in range(0, depth, tile):
        cols = slice(at, at + tile)
        after[:, cols] = hidden[:, cols].astype(jnp.float32) + jnp.dot(
            attended_ref[...], joined(full_a_ref, at // tile), preferred_element_type=jnp.float32
        )
    conv_rows[0, margin : margin + rows, :] = layer_norm(after[...]).astype(jnp.bfloat16)

    rows_copy = pltpu.make_async_remote_copy(
        src_ref=conv_rows.at[0, pl.ds(margin, rows), :],
        dst_ref=conv_rows.at[1, pl.ds(margin, rows), :],
        send_sem=rows_send,
        recv_sem=rows_recv,
        device_id={"seq": partner},
        device_id_type=MESH,
    )
    rows_copy.start()

    def edge_copy(side, slot):
        owner = lax.rem(me + (1 if side == 0 else shards - 1), shards)
        first, at = (rows, 0) if side == 0 else (margin, margin + rows)
        return pltpu.make_async_remote_copy(
            src_ref=conv_rows.at[0, pl.ds(first, margin), :],
            dst_ref=conv_rows.at[slot, pl.ds(at, margin), :],
            send_sem=edge_send.at[side, slot],
            recv_sem=edge_recv.at[side, slot],
            device_id={"seq": owner if slot == 0 else partner_of(owner)},
            device_id_type=MESH,
        )

    edges = [edge_copy(side, slot) for slot in range(2) for side in range(2)]
    for copy in edges:
        copy.start()
    for piece in range(2):
        b_copy(0, piece).wait_recv()
        b_copy(2, piece).start()
    send(2)
    kept[1].wait()
    rows_copy.wait_recv()
    for copy in edges:
        copy.wait_recv()

    part = w_b_ref.shape[1]
    reach = KERNEL // 2

    def gate(piece):
        for slot in range(2):
            block = conv_rows[slot]
            value = jnp.dot(block, half_b_ref[piece], preferred_element_type=jnp.float32)
            gates = jnp.dot(block, half_b_ref[2 + piece], preferred_element_type=jnp.float32)
            glu = (value * jax.nn.sigmoid(gates)).astype(jnp.bfloat16)
            padded[slot] = glu.astype(jnp.float32)

    def taps_of(piece, slot, at):
        cols = pl.ds(pl.multiple_of(half * (2 * part) + piece * part + at, 128), 128)
        block = taps[:, cols]
        own = near[slot, margin : margin + rows, :]
        summed = jnp.zeros((rows, 128), jnp.float32)
        for offset in range(KERNEL):
            start = margin - reach + offset
            term = padded[slot, start : start + rows, at : at + 128] * block[offset : offset + 1]
            keep = near[slot, start : start + rows, :] == own
            summed = summed + jnp.where(keep, term, 0.0)
        if slot == 0:
            depthwise[:, cols] = summed
        else:
            deep_out[:, pl.ds(pl.multiple_of(piece * part + at, 128), 128)] = summed.astype(
                jnp.bfloat16
            )

    def deep_copy(order):
        piece = odd if order == 0 else 1 - odd
        cols = pl.ds(pl.multiple_of(piece * part, 128), part)
        return pltpu.make_async_remote_copy(
            src_ref=deep_out.at[:, cols],
            dst_ref=deep_in.at[:, cols],
            send_sem=deep_send.at[order],
            recv_sem=deep_recv.at[order],
            device_id={"seq": partner},
            device_id_type=MESH,
        )

    def convolve(order):
        piece = odd if order == 0 else 1 - odd
        gate(piece)
        for at in range(0, part, 128):
            taps_of(piece, 1, at)
        deep_copy(order).start()
        for at in range(0, part, 128):
            taps_of(piece, 0, at)

    convolve(0)
    forward(2, 0)
    for kind in (1, 2):
        for piece in range(2):
            b_copy(kind, piece).wait_recv()
    convolve(1)
    forward(2, 1)
    for order in range(2):
        deep_copy(order).wait_recv()
    other = pl.ds(pl.multiple_of((1 - half) * (2 * part), 128), 2 * part)
    depthwise[:, other] = deep_in[...].astype(jnp.float32)
    conv_act = layer_norm(depthwise[...])
    conv_act = (conv_act * jax.nn.sigmoid(conv_act)).astype(jnp.bfloat16)

    def leave(piece, owner):
        cols = pl.ds(pl.multiple_of(owner * width, 128), width)
        return pltpu.make_async_remote_copy(
            src_ref=leaving.at[:, cols],
            dst_ref=handed_ref.at[:, cols],
            send_sem=leave_send.at[piece],
            recv_sem=leave_recv.at[piece],
            device_id={"phase": phase_next},
            device_id_type=MESH,
        )

    sent = []

    def finish(owner):
        cols = pl.ds(pl.multiple_of(owner * width, 128), width)
        leaving[:, cols] = (
            after[:, cols]
            + jnp.dot(conv_act, full_c_ref[owner], preferred_element_type=jnp.float32)
        ).astype(jnp.bfloat16)
        copy = leave(len(sent), owner)
        copy.start()
        sent.append(copy)

    kept[2].wait()
    finish(me)
    for step in range(steps):
        if step >= 2:
            forward(2, step)
        finish(ring_index(place - 1 - step, shards))
        if step < steps - 1:
            finish(ring_index(place + 1 + step, shards))
    for away in range(1, shards):
        out_copy(away).wait_send()
    rows_copy.wait_send()
    for copy in edges:
        copy.wait_send()
    for order in range(2):
        deep_copy(order).wait_send()
    for kind in range(3):
        for piece in range(2):
            b_copy(kind, piece).wait_send()
    for load in range(3):
        for step in range(steps):
            for way, piece in hops(step):
                hop(load, step, way, piece).wait_send()
    for copy in sent:
        copy.wait()


def block_call(shards, hidden, lengths, taps, weights):
    rows, depth = hidden.shape
    width = weights[0].shape[1]
    part = weights[4].shape[1]
    total = rows * shards
    steps = shards // 2
    margin = 16
    vmem = pl.BlockSpec(memory_space=pltpu.VMEM)
    smem = pl.BlockSpec(memory_space=pltpu.SMEM)
    anywhere = pl.BlockSpec(memory_space=pl.ANY)
    dma = pltpu.SemaphoreType.DMA
    bf16, f32 = jnp.bfloat16, jnp.float32
    return pl.pallas_call(
        functools.partial(block_kernel, shards, depth // HEADS),
        out_shape=jax.ShapeDtypeStruct((rows, depth), bf16),
        in_specs=[smem, anywhere, vmem] + [anywhere] * 6,
        out_specs=vmem,
        scratch_shapes=[
            pltpu.VMEM((rows, depth), bf16),
            pltpu.VMEM((depth, 3 * width), bf16),
            pltpu.VMEM((shards, depth, width), bf16),
            pltpu.VMEM((shards // 2, depth, part), bf16),
            pltpu.VMEM((shards, depth, width), bf16),
            pltpu.VMEM((rows, depth), bf16),
            pltpu.VMEM((rows, depth), f32),
            pltpu.VMEM((2, rows + 2 * margin, depth), bf16),
            pltpu.VMEM((2, rows + 2 * margin, 128), jnp.int32),
            pltpu.VMEM(taps.shape, f32),
            pltpu.VMEM((2, rows + 2 * margin, part), f32),
            pltpu.VMEM((rows, depth), f32),
            pltpu.VMEM((rows, depth // 2), bf16),
            pltpu.VMEM((rows, depth // 2), bf16),
            pltpu.VMEM((rows, depth), bf16),
            pltpu.VMEM((total, depth), bf16),
            pltpu.VMEM((total, width), bf16),
            pltpu.VMEM((total, width), bf16),
            pltpu.VMEM((total, width), bf16),
            pltpu.VMEM((shards - 1, rows, width), bf16),
            dma((3 * steps * 2, 2)),
            dma((3 * steps * 2, 2)),
            dma((3,)),
            dma((shards - 1,)),
            dma((shards - 1,)),
            dma((4,)),
            dma((3, 2)),
            dma((3, 2)),
            dma,
            dma,
            dma((2, 2)),
            dma((2, 2)),
            dma((2,)),
            dma((2,)),
            dma((shards,)),
            dma((shards,)),
        ],
        compiler_params=pltpu.CompilerParams(
            collective_id=0, has_side_effects=True, vmem_limit_bytes=56 * 1024 * 1024
        ),
    )(lengths, hidden, taps, *weights)


def attention_general(hidden, utt_lengths, w_query, w_key, w_value, w_output, conv_in, conv_out):
    shards = lax.axis_size("seq")
    my_index = lax.axis_index("seq")
    local_rows = hidden.shape[0]
    width = hidden.shape[1]
    total_rows = local_rows * shards
    head_size = width // HEADS
    scale = 1.0 / math.sqrt(head_size)
    groups = min(HEADS, shards)
    group_heads = HEADS // groups
    parts = shards // groups
    part_rows = local_rows // parts
    group_width = group_heads * head_size
    full_query, full_key, full_value, full_output, full_conv_in, full_conv_out = (
        lax.all_gather(w_query, "seq", axis=1, tiled=True),
        lax.all_gather(w_key, "seq", axis=1, tiled=True),
        lax.all_gather(w_value, "seq", axis=1, tiled=True),
        lax.all_gather(w_output, "seq", axis=1, tiled=True),
        lax.all_gather(conv_in, "seq", axis=1, tiled=True),
        lax.all_gather(conv_out, "seq", axis=1, tiled=True),
    )
    normed = layer_norm(hidden.astype(jnp.float32)).astype(jnp.bfloat16)
    query = jnp.dot(normed, full_query, preferred_element_type=jnp.float32).astype(jnp.bfloat16)
    key_proj = jnp.dot(normed, full_key, preferred_element_type=jnp.float32).astype(jnp.bfloat16)
    value_proj = jnp.dot(normed, full_value, preferred_element_type=jnp.float32).astype(
        jnp.bfloat16
    )
    shaped = query.reshape(parts, part_rows, groups, group_width).transpose(2, 0, 1, 3)
    query_pieces = shaped.reshape(shards, part_rows, group_width)
    kv_local = jnp.concatenate(
        [
            key_proj.reshape(local_rows, groups, group_width),
            value_proj.reshape(local_rows, groups, group_width),
        ],
        axis=2,
    )
    copies = jnp.broadcast_to(
        kv_local.transpose(1, 0, 2)[:, None], (groups, parts, local_rows, 2 * group_width)
    )
    copies = copies.reshape(shards, local_rows, 2 * group_width)
    query_got, kv_got = (
        lax.all_to_all(query_pieces, "seq", split_axis=0, concat_axis=0, tiled=True),
        lax.all_to_all(copies, "seq", split_axis=0, concat_axis=0, tiled=True),
    )
    key_value = kv_got.reshape(total_rows, 2 * group_width)
    count = shards * part_rows
    my_part = my_index % parts
    row_ids = jnp.arange(count, dtype=jnp.int32)
    query_pos = row_ids // part_rows * local_rows + my_part * part_rows + row_ids % part_rows
    queries = query_got.reshape(count, group_heads, head_size)
    key_rows = key_value[:, :group_width].reshape(total_rows, group_heads, head_size)
    value_rows = key_value[:, group_width:].reshape(total_rows, group_heads, head_size)
    seg_all = segment_ids(jnp.arange(total_rows, dtype=jnp.int32), utt_lengths)
    seg_query = segment_ids(query_pos, utt_lengths)
    query_block = math.gcd(512, count)
    blocks = count // query_block

    def attend_block(operands):
        block_query, block_seg = operands
        scores = (
            jnp.einsum("qhd,khd->hqk", block_query, key_rows, preferred_element_type=jnp.float32)
            * scale
        )
        allowed = (block_seg[:, None] == seg_all[None, :])[None]
        scores = jnp.where(allowed, scores, -1e30)
        peak = jnp.max(scores, axis=2, keepdims=True)
        expw = jnp.where(allowed, jnp.exp(scores - peak), 0.0)
        total_weight = jnp.sum(expw, axis=2)
        mixed = jnp.einsum(
            "hqk,khd->hqd",
            expw.astype(jnp.bfloat16),
            value_rows,
            preferred_element_type=jnp.float32,
        )
        mixed = mixed / total_weight[:, :, None]
        return mixed.transpose(1, 0, 2).astype(jnp.bfloat16)

    attended = lax.map(
        attend_block,
        (
            queries.reshape(blocks, query_block, group_heads, head_size),
            seg_query.reshape(blocks, query_block),
        ),
    )
    outgoing = attended.reshape(shards, part_rows, group_width)
    returned = lax.all_to_all(outgoing, "seq", split_axis=0, concat_axis=0, tiled=True)
    attended_local = (
        returned.reshape(groups, parts, part_rows, group_width)
        .transpose(1, 2, 0, 3)
        .reshape(local_rows, width)
    )
    return attended_local, full_output, full_conv_in, full_conv_out


def body(frames, lengths, w_query, w_key, w_value, w_output, conv_in, conv_taps, conv_out):
    hidden = frames[0]
    utt_lengths = lengths[0]
    shards = lax.axis_size("seq")
    my_index = lax.axis_index("seq")
    local_rows = hidden.shape[0]
    width = hidden.shape[1]
    total_rows = local_rows * shards
    phases = lax.axis_size("phase")
    if phases > 2 and shards == 8 and width // shards == 128 and local_rows % 32 == 0:
        weights = (w_query[0], w_key[0], w_value[0], w_output[0], conv_in[0], conv_out[0])
        return block_call(shards, hidden, utt_lengths, conv_taps[0], weights)[None]
    attended_local, full_output, full_conv_in, full_conv_out = attention_general(
        hidden, utt_lengths, w_query[0], w_key[0], w_value[0], w_output[0], conv_in[0], conv_out[0]
    )
    after_attn = hidden.astype(jnp.float32) + jnp.dot(
        attended_local, full_output, preferred_element_type=jnp.float32
    )
    conv_normed = layer_norm(after_attn).astype(jnp.bfloat16)
    gates = jnp.dot(conv_normed, full_conv_in, preferred_element_type=jnp.float32)
    glu = (gates[:, :width] * jax.nn.sigmoid(gates[:, width:])).astype(jnp.bfloat16)
    reach = KERNEL // 2
    padded = padded_2(glu, (("seq", 0),), KERNEL // 2)
    padded_pos = my_index * local_rows - reach + jnp.arange(local_rows + 2 * reach, dtype=jnp.int32)
    inside = (padded_pos >= 0) & (padded_pos < total_rows)
    padded_seg = jnp.where(inside, segment_ids(padded_pos, utt_lengths), -1)
    own_seg = padded_seg[reach : reach + local_rows]
    taps = conv_taps[0]
    depthwise = jnp.zeros((local_rows, width), jnp.float32)
    for offset in range(KERNEL):
        keep = padded_seg[offset : offset + local_rows] == own_seg
        term = padded[offset : offset + local_rows].astype(jnp.float32) * taps[offset].astype(
            jnp.float32
        )
        depthwise = depthwise + jnp.where(keep[:, None], term, 0.0)
    conv_act = layer_norm(depthwise)
    conv_act = (conv_act * jax.nn.sigmoid(conv_act)).astype(jnp.bfloat16)
    block_out = (
        after_attn + jnp.dot(conv_act, full_conv_out, preferred_element_type=jnp.float32)
    ).astype(jnp.bfloat16)
    passed = passed_along(block_out, "phase", 1)
    return passed[None]


def solution(mesh):
    in_specs = (
        P("phase", "seq", None),
        P("phase", None),
        P("phase", None, "seq"),
        P("phase", None, "seq"),
        P("phase", None, "seq"),
        P("phase", None, "seq"),
        P("phase", None, "seq"),
        P("phase", None, None),
        P("phase", None, "seq"),
    )
    out_specs = P("phase", "seq", None)
    return jax.shard_map(body, mesh=mesh, in_specs=in_specs, out_specs=out_specs, check_vma=False)
```

```python
import functools
import math

import jax
import jax.numpy as jnp
from jax import lax
from jax.experimental import pallas as pl
from jax.experimental.pallas import tpu as pltpu
from jax.sharding import PartitionSpec as P

HEADS = 16
KERNEL = 31
MESH = pl.DeviceIdType.MESH


def padded_2(block, sides, width):
    for axis, dim in sides:
        count = lax.axis_size(axis)
        forward = [(i, i + 1) for i in range(count - 1)]
        backward = [(target, source) for source, target in forward]
        low = lax.ppermute(
            lax.slice_in_dim(block, block.shape[dim] - width, None, axis=dim), axis, forward
        )
        high = lax.ppermute(lax.slice_in_dim(block, 0, width, axis=dim), axis, backward)
        block = jnp.concatenate([low, block, high], axis=dim)
    return block


def passed_along(block, axis, distance):
    devices = range(lax.axis_size(axis))
    route = [((i - distance) % len(devices), i) for i in devices]
    return lax.ppermute(block, axis, route)


def layer_norm(values):
    centre = values - jnp.mean(values, axis=-1, keepdims=True)
    spread = jnp.mean(centre * centre, axis=-1, keepdims=True)
    return centre * lax.rsqrt(spread + 1e-05)


def segment_ids(positions, lengths):
    order = jnp.arange(lengths.shape[0], dtype=jnp.int32)
    bounds = jnp.sum(jnp.where(order[None, :] <= order[:, None], lengths[None, :], 0), axis=1)
    return jnp.sum((positions[:, None] >= bounds[None, :]).astype(jnp.int32), axis=1)


def ring_index(place, shards):
    place = lax.rem(place + shards, shards)
    late = lax.div(place, shards // 2)
    return (1 - late) * (2 * place) + late * (2 * (shards - 1 - place) + 1)


def segment_of(positions, bounds):
    segment = jnp.zeros(positions.shape, jnp.int32)
    for bound in bounds:
        segment = segment + (positions >= bound).astype(jnp.int32)
    return segment


def block_kernel(
    shards,
    head_size,
    lengths_ref,
    frames_ref,
    taps_ref,
    query_ref,
    key_ref,
    value_ref,
    w_a_ref,
    w_b_ref,
    w_c_ref,
    handed_ref,
    hidden,
    qkv,
    full_a_ref,
    half_b_ref,
    full_c_ref,
    attended_ref,
    after,
    conv_rows,
    near,
    taps,
    padded,
    depthwise,
    deep_out,
    deep_in,
    conv_act,
    leaving,
    normed,
    query,
    keys,
    values,
    outbox,
    send_sem,
    recv_sem,
    own_sem,
    out_send,
    out_recv,
    in_sem,
    w_send,
    w_recv,
    b_send,
    b_recv,
    hidden_send,
    hidden_recv,
    rows_send,
    rows_recv,
    edge_send,
    edge_recv,
    deep_send,
    deep_recv,
    leave_send,
    leave_recv,
):
    rows = frames_ref.shape[0]
    depth = frames_ref.shape[1]
    width = query_ref.shape[1]
    part = w_b_ref.shape[1]
    loads_in = [pltpu.make_async_copy(frames_ref, hidden.at[pl.ds(0, rows), :], in_sem.at[3])]
    for i, ref in enumerate((query_ref, key_ref, value_ref)):
        loads_in.append(
            pltpu.make_async_copy(ref, qkv.at[:, pl.ds(i * width, width)], in_sem.at[i])
        )
    for copy in loads_in:
        copy.start()
    steps = shards // 2
    me = lax.axis_index("seq")
    odd = lax.rem(me, 2)
    place = (1 - odd) * lax.div(me, 2) + odd * (shards - 1 - lax.div(me, 2))
    right, left = ring_index(place + 1, shards), ring_index(place - 1, shards)
    half = lax.rem(lax.div(me, 2), 2)
    upper = lax.div(me, 4)

    def partner_of(owner):
        return owner + 2 - 4 * lax.rem(lax.div(owner, 2), 2)

    def inner_of(owner):
        return lax.rem(lax.div(lax.div(owner, 2) + 1, 2), 2)

    beside = me + 1 - 2 * odd
    across = me + 4 - 8 * upper
    facing = me + 2 - 4 * upper
    partner = partner_of(me)
    inner = inner_of(me) == 1
    outer = inner_of(me) == 0
    home = inner_of(me) * me + (1 - inner_of(me)) * partner

    barrier = pltpu.get_barrier_semaphore()
    for away in range(1, shards):
        peer = lax.rem(me + away, shards)
        pl.semaphore_signal(barrier, inc=1, device_id={"seq": peer}, device_id_type=MESH)
    phase = lax.axis_index("phase")
    phases = lax.axis_size("phase")
    phase_next = lax.rem(phase + 1, phases)
    phase_back = lax.rem(phase + phases - 1, phases)
    for other in (phase_next, phase_back):
        for peer in (me, partner):
            pl.semaphore_signal(
                barrier, inc=1, device_id={"phase": other, "seq": peer}, device_id_type=MESH
            )

    loads_in[0].wait()
    own_rows = pl.ds(pl.multiple_of(me * rows, rows), rows)
    normed[own_rows, :] = layer_norm(hidden[:rows, :].astype(jnp.float32)).astype(jnp.bfloat16)
    pl.semaphore_wait(barrier, shards + 3)

    def remote(source, target, sent, got, peer, onward=None):
        place_of = {"seq": peer} if onward is None else {"phase": onward, "seq": peer}
        return pltpu.make_async_remote_copy(
            src_ref=source,
            dst_ref=target,
            send_sem=sent,
            recv_sem=got,
            device_id=place_of,
            device_id_type=MESH,
        )

    def hop(step, way, piece):
        owner = ring_index(place - step if way == 0 else place + step, shards)
        size = rows // 2
        block = normed.at[pl.ds(pl.multiple_of(owner * rows + piece * size, 16), size), :]
        at = step * 2 + way
        peer = right if way == 0 else left
        return remote(block, block, send_sem.at[at, piece], recv_sem.at[at, piece], peer)

    def hops(step):
        pairs = [(way, piece) for piece in range(2) for way in range(2)]
        return [(way, piece) for way, piece in pairs if step < steps - 1 or way == piece]

    def forward(step):
        onward = hops(step + 1) if step < steps - 1 else ()
        for way, piece in hops(step):
            hop(step, way, piece).wait_recv()
            if (way, piece) in onward:
                hop(step + 1, way, piece).start()

    def project(owner):
        at = pl.ds(pl.multiple_of(owner * rows, rows), rows)
        block = normed[at, :]
        both = jnp.dot(block, qkv[...], preferred_element_type=jnp.float32).astype(jnp.bfloat16)
        query[at, :] = both[:, :width] * jnp.bfloat16(1.0 / math.sqrt(head_size))
        keys[at, :] = both[:, width : 2 * width]
        values[at, :] = both[:, 2 * width :]

    fulls = ((w_a_ref, full_a_ref), (w_c_ref, full_c_ref))
    wholes = range(2)

    def chunk(full, owner, first, size):
        cols = pl.ds(pl.multiple_of(lax.rem(owner, 2) * width, 128), width)
        return full.at[lax.div(owner, 2), pl.ds(first, size), cols]

    def w_copy(load, kind, piece):
        own, full = fulls[load]
        size = depth // 2
        owner = (me, me, me, partner, partner, facing, partner_of(facing))[kind]
        peer = (partner, beside, facing, facing, beside, beside, beside)[kind]
        target = chunk(full, owner, piece * size, size)
        source = own.at[pl.ds(piece * size, size), :] if kind < 3 else target
        return remote(
            source, target, w_send.at[load, kind, piece], w_recv.at[load, kind, piece], peer
        )

    def w_start(load, kind):
        for piece in wholes:
            w_copy(load, kind, piece).start()

    def w_wait(load, kind, then=()):
        for piece in wholes:
            w_copy(load, kind, piece).wait_recv()
            for more in then:
                w_copy(load, more, piece).start()

    def b_slot(owner):
        return lax.div(owner, 4) * 2 + lax.rem(owner, 2)

    b_pieces = range(4)

    def b_copy(kind, piece):
        size = depth // len(b_pieces)
        at = pl.ds(piece * size, size)
        target = half_b_ref.at[b_slot(across if kind == 2 else me), at, :]
        source = target if kind == 2 else w_b_ref.at[at, :]
        peer = across if kind == 0 else beside
        return remote(source, target, b_send.at[kind, piece], b_recv.at[kind, piece], peer)

    def b_start(kind):
        for piece in b_pieces:
            b_copy(kind, piece).start()

    for way, piece in hops(0):
        hop(0, way, piece).start()

    @pl.when(inner)
    def _():
        w_start(0, 1)
        b_start(1)

    kept = [
        pltpu.make_async_copy(w_a_ref, chunk(full_a_ref, me, 0, depth), own_sem.at[0]),
        pltpu.make_async_copy(w_b_ref, half_b_ref.at[b_slot(me)], own_sem.at[1]),
        pltpu.make_async_copy(w_c_ref, chunk(full_c_ref, me, 0, depth), own_sem.at[2]),
    ]
    for copy in kept:
        copy.start()
    hidden_copy = remote(
        hidden.at[pl.ds(0, rows), :],
        hidden.at[pl.ds(rows, rows), :],
        hidden_send,
        hidden_recv,
        partner,
    )

    bounds = [lengths_ref[0]]
    for utt in range(1, lengths_ref.shape[0]):
        bounds.append(bounds[-1] + lengths_ref[utt])
    seg_col = segment_of(lax.broadcasted_iota(jnp.int32, (1, rows * shards), 1), bounds)
    margin = (near.shape[1] - rows) // 2
    for slot, owner in enumerate((me, partner)):
        positions = lax.broadcasted_iota(jnp.int32, near.shape[1:], 0) + (owner * rows - margin)
        near[slot] = jnp.where(positions >= 0, segment_of(positions, bounds), -1)
    taps[...] = taps_ref[...].astype(jnp.float32)

    for copy in loads_in[1:]:
        copy.wait()
    project(me)
    for step in range(steps):
        forward(step)
        if step == steps - 2:

            @pl.when(outer)
            def _():
                w_start(0, 0)
                hidden_copy.start()

            @pl.when(inner)
            def _():
                w_start(0, 2)

        project(ring_index(place - 1 - step, shards))
        if step < steps - 1:
            project(ring_index(place + 1 + step, shards))

    lane = lax.broadcasted_iota(jnp.int32, (rows, width), 1)
    my_columns = pl.ds(pl.multiple_of(me * width, 128), width)

    def attend(owner):
        at = pl.ds(pl.multiple_of(owner * rows, rows), rows)
        block = query[at, :]
        positions = lax.broadcasted_iota(jnp.int32, (rows, 1), 0) + owner * rows
        allowed = segment_of(positions, bounds) == seg_col
        result = jnp.zeros((rows, width), jnp.float32)
        for head in range(width // head_size):
            mine = (lane >= head * head_size) & (lane < (head + 1) * head_size)
            scores = lax.dot_general(
                jnp.where(mine, block, jnp.bfloat16(0)),
                keys[...],
                (((1,), (1,)), ((), ())),
                preferred_element_type=jnp.float32,
            )
            scores = jnp.where(allowed, scores, -1e30)
            peak = jnp.max(scores, axis=1, keepdims=True)
            expw = jnp.exp(scores - peak)
            total = jnp.sum(expw, axis=1, keepdims=True)
            mixed = jnp.dot(
                expw.astype(jnp.bfloat16), values[...], preferred_element_type=jnp.float32
            )
            result = jnp.where(mine, mixed / total, result)
        return result.astype(jnp.bfloat16)

    def out_copy(turn, target):
        return remote(
            outbox.at[turn],
            attended_ref.at[:, my_columns],
            out_send.at[turn],
            out_recv.at[me],
            target,
        )

    turns = steps

    def target_of(turn):
        return 2 + lax.rem(home - 2 + 1 + turn, turns)

    for turn in range(turns):
        target = target_of(turn)
        outbox[turn, :rows, :] = attend(target)
        outbox[turn, rows:, :] = attend(partner_of(target))
        if turn < turns - 1:
            out_copy(turn, target).start()
        else:

            @pl.when(outer)
            def _():
                out_copy(turns - 1, partner).start()

            @pl.when(inner)
            def _():
                attended_ref[:, my_columns] = outbox[turns - 1]

        if turn == 2:

            @pl.when(inner)
            def _():
                w_wait(0, 0, (3, 4))
                w_wait(0, 2, (5,))

    b_start(0)

    @pl.when(outer)
    def _():
        b_start(1)

    def rows_copy(slot):
        return remote(
            conv_rows.at[slot, pl.ds(margin, rows), :],
            conv_rows.at[1 - slot, pl.ds(margin, rows), :],
            rows_send.at[slot],
            rows_recv.at[slot],
            partner,
        )

    def edge_copy(slot, side, deep):
        source = me if slot == 0 else partner
        owner = lax.rem(source + (1 if side == 0 else shards - 1), shards)
        is_inner = inner_of(owner)
        first, at = (rows, 0) if side == 0 else (margin, margin + rows)
        peer = is_inner * owner + (1 - is_inner) * partner_of(owner)
        where = 1 - is_inner
        if deep == 1:
            peer, where = partner_of(peer), is_inner
        return remote(
            conv_rows.at[slot, pl.ds(first, margin), :],
            conv_rows.at[where, pl.ds(at, margin), :],
            edge_send.at[slot, side, deep],
            edge_recv.at[where, side],
            peer,
        )

    def edge_arrival(slot, side):
        at = 0 if side == 0 else margin + rows
        block = conv_rows.at[slot, pl.ds(at, margin), :]
        return remote(block, block, edge_send.at[0, 0, 0], edge_recv.at[slot, side], partner)

    @pl.when(inner)
    def _():
        w_wait(0, 3, (6,))
        for away in range(1, shards):
            source = lax.rem(me + away, shards)
            remote(
                outbox.at[0],
                attended_ref.at[:, my_columns],
                out_send.at[0],
                out_recv.at[source],
                source,
            ).wait_recv()
        hidden_copy.wait_recv()
        kept[0].wait()

        def output_part(owner):
            at = lax.div(owner, 2)
            cols = pl.ds(pl.multiple_of(at * (2 * width), 128), 2 * width)
            after[:, cols] = hidden[:, cols].astype(jnp.float32) + jnp.dot(
                attended_ref[...], full_a_ref[at], preferred_element_type=jnp.float32
            )

        w_wait(0, 1)
        output_part(me)
        w_wait(0, 4)
        output_part(partner)
        w_wait(0, 5)
        output_part(facing)
        w_wait(0, 6)
        output_part(partner_of(facing))
        for slot in (1, 0):
            block = layer_norm(after[slot * rows : (slot + 1) * rows, :]).astype(jnp.bfloat16)
            conv_rows[slot, margin : margin + rows, :] = block
            for side in range(2):
                for deep in range(2):
                    edge_copy(slot, side, deep).start()
            rows_copy(slot).start()

    for piece in b_pieces:
        b_copy(0, piece).wait_recv()
        b_copy(2, piece).start()

    @pl.when(inner)
    def _():
        w_start(1, 1)
        w_start(1, 2)

    @pl.when(outer)
    def _():
        kept[0].wait()
        w_start(1, 0)
        for slot in range(2):
            rows_copy(slot).wait_recv()

    kept[1].wait()
    kept[2].wait()
    for slot in range(2):
        for side in range(2):
            edge_arrival(slot, side).wait_recv()

    reach = KERNEL // 2

    def gate(piece):
        for slot in range(2):
            block = conv_rows[slot]
            value = jnp.dot(block, half_b_ref[piece], preferred_element_type=jnp.float32)
            gates = jnp.dot(block, half_b_ref[2 + piece], preferred_element_type=jnp.float32)
            glu = (value * jax.nn.sigmoid(gates)).astype(jnp.bfloat16)
            padded[slot] = glu.astype(jnp.float32)

    def taps_of(piece, slot, at):
        cols = pl.ds(pl.multiple_of(half * (2 * part) + piece * part + at, 128), 128)
        block = taps[:, cols]
        own = near[slot, margin : margin + rows, :]
        summed = jnp.zeros((rows, 128), jnp.float32)
        for offset in range(KERNEL):
            start = margin - reach + offset
            term = padded[slot, start : start + rows, at : at + 128] * block[offset : offset + 1]
            keep = near[slot, start : start + rows, :] == own
            summed = summed + jnp.where(keep, term, 0.0)
        depthwise[slot * rows : (slot + 1) * rows, cols] = summed
        deep_cols = pl.ds(pl.multiple_of(piece * part + at, 128), 128)
        deep_out[slot, :, deep_cols] = summed.astype(jnp.bfloat16)

    def deep_copy(order, slot):
        piece = odd if order == 0 else 1 - odd
        cols = pl.ds(pl.multiple_of(piece * part, 128), part)
        return remote(
            deep_out.at[slot, :, cols],
            deep_in.at[1 - slot, :, cols],
            deep_send.at[order, slot],
            deep_recv.at[order, slot],
            partner,
        )

    def convolve(order):
        piece = odd if order == 0 else 1 - odd
        gate(piece)
        for slot in range(2):
            for at in range(0, part, 128):
                taps_of(piece, slot, at)

            @pl.when(outer)
            def _():
                deep_copy(order, slot).start()

    convolve(0)

    @pl.when(inner)
    def _():
        w_wait(1, 0, (3, 4))
        w_wait(1, 2, (5,))

    for kind in (1, 2):
        for piece in b_pieces:
            b_copy(kind, piece).wait_recv()
    convolve(1)

    def leave(turn, slot, owner):
        cols = pl.ds(pl.multiple_of(lax.div(owner, 2) * (2 * width), 128), 2 * width)
        return remote(
            leaving.at[pl.ds(slot * rows, rows), cols],
            handed_ref.at[:, cols],
            leave_send.at[turn, slot],
            leave_recv.at[turn],
            me if slot == 0 else partner,
            phase_next,
        )

    ends = (me, partner, facing, partner_of(facing))

    @pl.when(inner)
    def _():
        w_wait(1, 3, (6,))
        for order in range(2):
            for slot in range(2):
                deep_copy(order, slot).wait_recv()
        other = pl.ds(pl.multiple_of((1 - half) * (2 * part), 128), 2 * part)
        for slot in range(2):
            at = slice(slot * rows, (slot + 1) * rows)
            depthwise[at, other] = deep_in[slot].astype(jnp.float32)
            block = layer_norm(depthwise[at, :])
            conv_act[at, :] = (block * jax.nn.sigmoid(block)).astype(jnp.bfloat16)
        for turn, owner in enumerate(ends):
            for kind in ((1,), (4,), (5,), (6,))[turn]:
                w_wait(1, kind)
            at = lax.div(owner, 2)
            cols = pl.ds(pl.multiple_of(at * (2 * width), 128), 2 * width)
            leaving[:, cols] = (
                after[:, cols]
                + jnp.dot(conv_act[...], full_c_ref[at], preferred_element_type=jnp.float32)
            ).astype(jnp.bfloat16)
            for slot in (1, 0):
                leave(turn, slot, owner).start()

    for step in range(steps):
        for way, piece in hops(step):
            hop(step, way, piece).wait_send()
    for turn in range(turns - 1):
        out_copy(turn, target_of(turn)).wait_send()
    for kind in range(3):
        for piece in b_pieces:
            b_copy(kind, piece).wait_send()

    @pl.when(outer)
    def _():
        out_copy(turns - 1, partner).wait_send()
        hidden_copy.wait_send()
        for load in range(2):
            for piece in wholes:
                w_copy(load, 0, piece).wait_send()
        for order in range(2):
            for slot in range(2):
                deep_copy(order, slot).wait_send()

    @pl.when(inner)
    def _():
        for load in range(2):
            for kind in range(1, 7):
                for piece in wholes:
                    w_copy(load, kind, piece).wait_send()
        for slot in range(2):
            rows_copy(slot).wait_send()
            for side in range(2):
                for deep in range(2):
                    edge_copy(slot, side, deep).wait_send()
        for turn, owner in enumerate(ends):
            for slot in range(2):
                leave(turn, slot, owner).wait_send()

    for turn, owner in enumerate(ends):
        leave(turn, 0, owner).wait_recv()


def block_call(shards, hidden, lengths, taps, weights):
    rows, depth = hidden.shape
    width = weights[0].shape[1]
    part = weights[4].shape[1]
    total = rows * shards
    steps = shards // 2
    margin = 16
    vmem = pl.BlockSpec(memory_space=pltpu.VMEM)
    smem = pl.BlockSpec(memory_space=pltpu.SMEM)
    anywhere = pl.BlockSpec(memory_space=pl.ANY)
    dma = pltpu.SemaphoreType.DMA
    bf16, f32 = jnp.bfloat16, jnp.float32
    return pl.pallas_call(
        functools.partial(block_kernel, shards, depth // HEADS),
        out_shape=jax.ShapeDtypeStruct((rows, depth), bf16),
        in_specs=[smem, anywhere, vmem] + [anywhere] * 6,
        out_specs=vmem,
        scratch_shapes=[
            pltpu.VMEM((2 * rows, depth), bf16),
            pltpu.VMEM((depth, 3 * width), bf16),
            pltpu.VMEM((shards // 2, depth, 2 * width), bf16),
            pltpu.VMEM((shards // 2, depth, part), bf16),
            pltpu.VMEM((shards // 2, depth, 2 * width), bf16),
            pltpu.VMEM((2 * rows, depth), bf16),
            pltpu.VMEM((2 * rows, depth), f32),
            pltpu.VMEM((2, rows + 2 * margin, depth), bf16),
            pltpu.VMEM((2, rows + 2 * margin, 128), jnp.int32),
            pltpu.VMEM(taps.shape, f32),
            pltpu.VMEM((2, rows + 2 * margin, part), f32),
            pltpu.VMEM((2 * rows, depth), f32),
            pltpu.VMEM((2, rows, depth // 2), bf16),
            pltpu.VMEM((2, rows, depth // 2), bf16),
            pltpu.VMEM((2 * rows, depth), bf16),
            pltpu.VMEM((2 * rows, depth), bf16),
            pltpu.VMEM((total, depth), bf16),
            pltpu.VMEM((total, width), bf16),
            pltpu.VMEM((total, width), bf16),
            pltpu.VMEM((total, width), bf16),
            pltpu.VMEM((steps, 2 * rows, width), bf16),
            dma((2 * steps, 2)),
            dma((2 * steps, 2)),
            dma((3,)),
            dma((steps,)),
            dma((shards,)),
            dma((4,)),
            dma((2, 7, 2)),
            dma((2, 7, 2)),
            dma((3, 4)),
            dma((3, 4)),
            dma,
            dma,
            dma((2,)),
            dma((2,)),
            dma((2, 2, 2)),
            dma((2, 2)),
            dma((2, 2)),
            dma((2, 2)),
            dma((steps, 2)),
            dma((steps,)),
        ],
        compiler_params=pltpu.CompilerParams(
            collective_id=0, has_side_effects=True, vmem_limit_bytes=56 * 1024 * 1024
        ),
    )(lengths, hidden, taps, *weights)


def attention_general(hidden, utt_lengths, w_query, w_key, w_value, w_output, conv_in, conv_out):
    shards = lax.axis_size("seq")
    my_index = lax.axis_index("seq")
    local_rows = hidden.shape[0]
    width = hidden.shape[1]
    total_rows = local_rows * shards
    head_size = width // HEADS
    scale = 1.0 / math.sqrt(head_size)
    groups = min(HEADS, shards)
    group_heads = HEADS // groups
    parts = shards // groups
    part_rows = local_rows // parts
    group_width = group_heads * head_size
    full_query, full_key, full_value, full_output, full_conv_in, full_conv_out = (
        lax.all_gather(w_query, "seq", axis=1, tiled=True),
        lax.all_gather(w_key, "seq", axis=1, tiled=True),
        lax.all_gather(w_value, "seq", axis=1, tiled=True),
        lax.all_gather(w_output, "seq", axis=1, tiled=True),
        lax.all_gather(conv_in, "seq", axis=1, tiled=True),
        lax.all_gather(conv_out, "seq", axis=1, tiled=True),
    )
    normed = layer_norm(hidden.astype(jnp.float32)).astype(jnp.bfloat16)
    query = jnp.dot(normed, full_query, preferred_element_type=jnp.float32).astype(jnp.bfloat16)
    key_proj = jnp.dot(normed, full_key, preferred_element_type=jnp.float32).astype(jnp.bfloat16)
    value_proj = jnp.dot(normed, full_value, preferred_element_type=jnp.float32).astype(
        jnp.bfloat16
    )
    shaped = query.reshape(parts, part_rows, groups, group_width).transpose(2, 0, 1, 3)
    query_pieces = shaped.reshape(shards, part_rows, group_width)
    kv_local = jnp.concatenate(
        [
            key_proj.reshape(local_rows, groups, group_width),
            value_proj.reshape(local_rows, groups, group_width),
        ],
        axis=2,
    )
    copies = jnp.broadcast_to(
        kv_local.transpose(1, 0, 2)[:, None], (groups, parts, local_rows, 2 * group_width)
    )
    copies = copies.reshape(shards, local_rows, 2 * group_width)
    query_got, kv_got = (
        lax.all_to_all(query_pieces, "seq", split_axis=0, concat_axis=0, tiled=True),
        lax.all_to_all(copies, "seq", split_axis=0, concat_axis=0, tiled=True),
    )
    key_value = kv_got.reshape(total_rows, 2 * group_width)
    count = shards * part_rows
    my_part = my_index % parts
    row_ids = jnp.arange(count, dtype=jnp.int32)
    query_pos = row_ids // part_rows * local_rows + my_part * part_rows + row_ids % part_rows
    queries = query_got.reshape(count, group_heads, head_size)
    key_rows = key_value[:, :group_width].reshape(total_rows, group_heads, head_size)
    value_rows = key_value[:, group_width:].reshape(total_rows, group_heads, head_size)
    seg_all = segment_ids(jnp.arange(total_rows, dtype=jnp.int32), utt_lengths)
    seg_query = segment_ids(query_pos, utt_lengths)
    query_block = math.gcd(512, count)
    blocks = count // query_block

    def attend_block(operands):
        block_query, block_seg = operands
        scores = (
            jnp.einsum("qhd,khd->hqk", block_query, key_rows, preferred_element_type=jnp.float32)
            * scale
        )
        allowed = (block_seg[:, None] == seg_all[None, :])[None]
        scores = jnp.where(allowed, scores, -1e30)
        peak = jnp.max(scores, axis=2, keepdims=True)
        expw = jnp.where(allowed, jnp.exp(scores - peak), 0.0)
        total_weight = jnp.sum(expw, axis=2)
        mixed = jnp.einsum(
            "hqk,khd->hqd",
            expw.astype(jnp.bfloat16),
            value_rows,
            preferred_element_type=jnp.float32,
        )
        mixed = mixed / total_weight[:, :, None]
        return mixed.transpose(1, 0, 2).astype(jnp.bfloat16)

    attended = lax.map(
        attend_block,
        (
            queries.reshape(blocks, query_block, group_heads, head_size),
            seg_query.reshape(blocks, query_block),
        ),
    )
    outgoing = attended.reshape(shards, part_rows, group_width)
    returned = lax.all_to_all(outgoing, "seq", split_axis=0, concat_axis=0, tiled=True)
    attended_local = (
        returned.reshape(groups, parts, part_rows, group_width)
        .transpose(1, 2, 0, 3)
        .reshape(local_rows, width)
    )
    return attended_local, full_output, full_conv_in, full_conv_out


def body(frames, lengths, w_query, w_key, w_value, w_output, conv_in, conv_taps, conv_out):
    hidden = frames[0]
    utt_lengths = lengths[0]
    shards = lax.axis_size("seq")
    my_index = lax.axis_index("seq")
    local_rows = hidden.shape[0]
    width = hidden.shape[1]
    total_rows = local_rows * shards
    phases = lax.axis_size("phase")
    if phases > 2 and shards == 8 and width // shards == 128 and local_rows % 32 == 0:
        weights = (w_query[0], w_key[0], w_value[0], w_output[0], conv_in[0], conv_out[0])
        return block_call(shards, hidden, utt_lengths, conv_taps[0], weights)[None]
    attended_local, full_output, full_conv_in, full_conv_out = attention_general(
        hidden, utt_lengths, w_query[0], w_key[0], w_value[0], w_output[0], conv_in[0], conv_out[0]
    )
    after_attn = hidden.astype(jnp.float32) + jnp.dot(
        attended_local, full_output, preferred_element_type=jnp.float32
    )
    conv_normed = layer_norm(after_attn).astype(jnp.bfloat16)
    gates = jnp.dot(conv_normed, full_conv_in, preferred_element_type=jnp.float32)
    glu = (gates[:, :width] * jax.nn.sigmoid(gates[:, width:])).astype(jnp.bfloat16)
    reach = KERNEL // 2
    padded = padded_2(glu, (("seq", 0),), KERNEL // 2)
    padded_pos = my_index * local_rows - reach + jnp.arange(local_rows + 2 * reach, dtype=jnp.int32)
    inside = (padded_pos >= 0) & (padded_pos < total_rows)
    padded_seg = jnp.where(inside, segment_ids(padded_pos, utt_lengths), -1)
    own_seg = padded_seg[reach : reach + local_rows]
    taps = conv_taps[0]
    depthwise = jnp.zeros((local_rows, width), jnp.float32)
    for offset in range(KERNEL):
        keep = padded_seg[offset : offset + local_rows] == own_seg
        term = padded[offset : offset + local_rows].astype(jnp.float32) * taps[offset].astype(
            jnp.float32
        )
        depthwise = depthwise + jnp.where(keep[:, None], term, 0.0)
    conv_act = layer_norm(depthwise)
    conv_act = (conv_act * jax.nn.sigmoid(conv_act)).astype(jnp.bfloat16)
    block_out = (
        after_attn + jnp.dot(conv_act, full_conv_out, preferred_element_type=jnp.float32)
    ).astype(jnp.bfloat16)
    passed = passed_along(block_out, "phase", 1)
    return passed[None]


def solution(mesh):
    in_specs = (
        P("phase", "seq", None),
        P("phase", None),
        P("phase", None, "seq"),
        P("phase", None, "seq"),
        P("phase", None, "seq"),
        P("phase", None, "seq"),
        P("phase", None, "seq"),
        P("phase", None, None),
        P("phase", None, "seq"),
    )
    out_specs = P("phase", "seq", None)
    return jax.shard_map(body, mesh=mesh, in_specs=in_specs, out_specs=out_specs, check_vma=False)
```

```python
import functools
import math

import jax
import jax.numpy as jnp
from jax import lax
from jax.experimental import pallas as pl
from jax.experimental.pallas import tpu as pltpu
from jax.sharding import PartitionSpec as P

HEADS = 16
KERNEL = 31
MESH = pl.DeviceIdType.MESH


def padded_2(block, sides, width):
    for axis, dim in sides:
        count = lax.axis_size(axis)
        forward = [(i, i + 1) for i in range(count - 1)]
        backward = [(target, source) for source, target in forward]
        low = lax.ppermute(
            lax.slice_in_dim(block, block.shape[dim] - width, None, axis=dim), axis, forward
        )
        high = lax.ppermute(lax.slice_in_dim(block, 0, width, axis=dim), axis, backward)
        block = jnp.concatenate([low, block, high], axis=dim)
    return block


def passed_along(block, axis, distance):
    devices = range(lax.axis_size(axis))
    route = [((i - distance) % len(devices), i) for i in devices]
    return lax.ppermute(block, axis, route)


def layer_norm(values):
    centre = values - jnp.mean(values, axis=-1, keepdims=True)
    spread = jnp.mean(centre * centre, axis=-1, keepdims=True)
    return centre * lax.rsqrt(spread + 1e-05)


def segment_ids(positions, lengths):
    order = jnp.arange(lengths.shape[0], dtype=jnp.int32)
    bounds = jnp.sum(jnp.where(order[None, :] <= order[:, None], lengths[None, :], 0), axis=1)
    return jnp.sum((positions[:, None] >= bounds[None, :]).astype(jnp.int32), axis=1)


def ring_index(place, shards):
    place = lax.rem(place + shards, shards)
    late = lax.div(place, shards // 2)
    return (1 - late) * (2 * place) + late * (2 * (shards - 1 - place) + 1)


def segment_of(positions, bounds):
    segment = jnp.zeros(positions.shape, jnp.int32)
    for bound in bounds:
        segment = segment + (positions >= bound).astype(jnp.int32)
    return segment


def block_kernel(
    shards,
    head_size,
    lengths_ref,
    frames_ref,
    taps_ref,
    query_ref,
    key_ref,
    value_ref,
    w_a_ref,
    w_b_ref,
    w_c_ref,
    handed_ref,
    hidden,
    qkv,
    full_a_ref,
    half_b_ref,
    full_c_ref,
    attended_ref,
    after,
    conv_rows,
    near,
    taps,
    padded,
    depthwise,
    deep_out,
    deep_in,
    leaving,
    query,
    keys,
    values,
    outbox,
    send_sem,
    recv_sem,
    own_sem,
    out_send,
    out_recv,
    in_sem,
    w_send,
    w_recv,
    rows_send,
    rows_recv,
    edge_send,
    edge_recv,
    deep_send,
    deep_recv,
    leave_send,
    leave_recv,
):
    rows = frames_ref.shape[0]
    depth = frames_ref.shape[1]
    width = query_ref.shape[1]
    part = w_b_ref.shape[1]
    me = lax.axis_index("seq")
    own_rows = pl.ds(pl.multiple_of(me * rows, rows), rows)
    loads_in = [pltpu.make_async_copy(frames_ref, hidden.at[own_rows, :], in_sem.at[3])]
    for i, ref in enumerate((query_ref, key_ref, value_ref)):
        loads_in.append(
            pltpu.make_async_copy(ref, qkv.at[:, pl.ds(i * width, width)], in_sem.at[i])
        )
    for copy in loads_in:
        copy.start()
    steps = shards // 2
    odd = lax.rem(me, 2)
    place = (1 - odd) * lax.div(me, 2) + odd * (shards - 1 - lax.div(me, 2))
    right, left = ring_index(place + 1, shards), ring_index(place - 1, shards)
    half = lax.rem(lax.div(me, 2), 2)
    upper = lax.div(me, 4)

    def partner_of(owner):
        return owner + 2 - 4 * lax.rem(lax.div(owner, 2), 2)

    def inner_of(owner):
        return lax.rem(lax.div(lax.div(owner, 2) + 1, 2), 2)

    beside = me + 1 - 2 * odd
    facing = me + 2 - 4 * upper
    partner = partner_of(me)
    inner = inner_of(me) == 1
    outer = inner_of(me) == 0
    home = inner_of(me) * me + (1 - inner_of(me)) * partner

    barrier = pltpu.get_barrier_semaphore()
    for away in range(1, shards):
        peer = lax.rem(me + away, shards)
        pl.semaphore_signal(barrier, inc=1, device_id={"seq": peer}, device_id_type=MESH)
    phase = lax.axis_index("phase")
    phases = lax.axis_size("phase")
    phase_next = lax.rem(phase + 1, phases)
    phase_back = lax.rem(phase + phases - 1, phases)
    for other in (phase_next, phase_back):
        for peer in (me, partner):
            pl.semaphore_signal(
                barrier, inc=1, device_id={"phase": other, "seq": peer}, device_id_type=MESH
            )

    loads_in[0].wait()
    pl.semaphore_wait(barrier, shards + 3)

    def remote(source, target, sent, got, peer, onward=None):
        place_of = {"seq": peer} if onward is None else {"phase": onward, "seq": peer}
        return pltpu.make_async_remote_copy(
            src_ref=source,
            dst_ref=target,
            send_sem=sent,
            recv_sem=got,
            device_id=place_of,
            device_id_type=MESH,
        )

    def hop(step, way, piece):
        owner = ring_index(place - step if way == 0 else place + step, shards)
        size = rows // 2
        block = hidden.at[pl.ds(pl.multiple_of(owner * rows + piece * size, 16), size), :]
        at = step * 2 + way
        peer = right if way == 0 else left
        return remote(block, block, send_sem.at[at, piece], recv_sem.at[at, piece], peer)

    def hops(step):
        pairs = [(way, piece) for piece in range(2) for way in range(2)]
        return [(way, piece) for way, piece in pairs if step < steps - 1 or way == piece]

    def forward(step):
        onward = hops(step + 1) if step < steps - 1 else ()
        for way, piece in hops(step):
            hop(step, way, piece).wait_recv()
            if (way, piece) in onward:
                hop(step + 1, way, piece).start()

    def project(owner):
        at = pl.ds(pl.multiple_of(owner * rows, rows), rows)
        block = layer_norm(hidden[at, :].astype(jnp.float32)).astype(jnp.bfloat16)
        both = jnp.dot(block, qkv[...], preferred_element_type=jnp.float32).astype(jnp.bfloat16)
        query[at, :] = both[:, :width] * jnp.bfloat16(1.0 / math.sqrt(head_size))
        keys[at, :] = both[:, width : 2 * width]
        values[at, :] = both[:, 2 * width :]

    fulls = ((w_a_ref, full_a_ref), (w_c_ref, full_c_ref), (w_b_ref, half_b_ref))
    wholes = range(2)

    def chunk(load, owner, first, size):
        full = fulls[load][1]
        if load == 2:
            return full.at[lax.div(owner, 2), pl.ds(first, size), :]
        cols = pl.ds(pl.multiple_of(lax.rem(owner, 2) * width, 128), width)
        return full.at[lax.div(owner, 2), pl.ds(first, size), cols]

    def w_copy(load, kind, piece):
        own = fulls[load][0]
        size = depth // 2
        owner = (me, me, me, partner, beside, facing, partner_of(facing), me)[kind]
        peer = (partner, beside, facing, facing, partner, beside, beside, beside)[kind]
        target = chunk(load, owner, piece * size, size)
        source = own.at[pl.ds(piece * size, size), :] if kind in (0, 1, 2, 7) else target
        return remote(
            source, target, w_send.at[load, kind, piece], w_recv.at[load, kind, piece], peer
        )

    def w_start(load, kind):
        for piece in wholes:
            w_copy(load, kind, piece).start()

    def w_wait(load, kind, then=()):
        for piece in wholes:
            w_copy(load, kind, piece).wait_recv()
            for more in then:
                w_copy(load, more, piece).start()

    for way, piece in hops(0):
        hop(0, way, piece).start()

    @pl.when(inner)
    def _():
        w_start(0, 1)
        w_start(1, 1)

    kept = [
        pltpu.make_async_copy(fulls[load][0], chunk(load, me, 0, depth), own_sem.at[load])
        for load in range(3)
    ]
    for copy in kept:
        copy.start()
    bounds = [lengths_ref[0]]
    for utt in range(1, lengths_ref.shape[0]):
        bounds.append(bounds[-1] + lengths_ref[utt])
    seg_col = segment_of(lax.broadcasted_iota(jnp.int32, (1, rows * shards), 1), bounds)
    margin = 16
    span = rows * steps
    first_row = upper * span
    for shift in range(near.shape[0]):
        positions = lax.broadcasted_iota(jnp.int32, near.shape[1:], 0)
        positions = positions + (first_row + shift - KERNEL // 2)
        near[shift] = jnp.where(positions >= 0, segment_of(positions, bounds), -1)
    outside = pl.multiple_of(upper * (span + margin), 16)
    conv_rows[pl.ds(outside, margin), :] = jnp.zeros((margin, depth), jnp.bfloat16)
    taps[...] = taps_ref[...].astype(jnp.float32)

    for copy in loads_in[1:]:
        copy.wait()
    project(me)
    for step in range(steps):
        forward(step)
        if step == steps - 2:

            @pl.when(outer)
            def _():
                w_start(0, 0)
                w_start(0, 7)

            @pl.when(inner)
            def _():
                w_start(0, 2)

        project(ring_index(place - 1 - step, shards))
        if step < steps - 1:
            project(ring_index(place + 1 + step, shards))

    lane = lax.broadcasted_iota(jnp.int32, (rows, width), 1)
    my_columns = pl.ds(pl.multiple_of(me * width, 128), width)

    def attend(owner):
        at = pl.ds(pl.multiple_of(owner * rows, rows), rows)
        block = query[at, :]
        positions = lax.broadcasted_iota(jnp.int32, (rows, 1), 0) + owner * rows
        allowed = segment_of(positions, bounds) == seg_col
        result = jnp.zeros((rows, width), jnp.float32)
        for head in range(width // head_size):
            mine = (lane >= head * head_size) & (lane < (head + 1) * head_size)
            scores = lax.dot_general(
                jnp.where(mine, block, jnp.bfloat16(0)),
                keys[...],
                (((1,), (1,)), ((), ())),
                preferred_element_type=jnp.float32,
            )
            scores = jnp.where(allowed, scores, -1e30)
            peak = jnp.max(scores, axis=1, keepdims=True)
            expw = jnp.exp(scores - peak)
            total = jnp.sum(expw, axis=1, keepdims=True)
            mixed = jnp.dot(
                expw.astype(jnp.bfloat16), values[...], preferred_element_type=jnp.float32
            )
            result = jnp.where(mine, mixed / total, result)
        return result.astype(jnp.bfloat16)

    def out_copy(turn, target):
        return remote(
            outbox.at[turn],
            attended_ref.at[:, my_columns],
            out_send.at[turn],
            out_recv.at[me],
            target,
        )

    turns = steps

    def target_of(turn):
        return 2 + lax.rem(home - 2 + 1 + turn, turns)

    for turn in range(turns):
        target = target_of(turn)
        outbox[turn, :rows, :] = attend(target)
        outbox[turn, rows:, :] = attend(partner_of(target))
        if turn < turns - 1:
            out_copy(turn, target).start()
        else:

            @pl.when(outer)
            def _():
                out_copy(turns - 1, partner).start()

            @pl.when(inner)
            def _():
                attended_ref[:, my_columns] = outbox[turns - 1]

        if turn == 2:

            @pl.when(inner)
            def _():
                w_wait(0, 0, (3,))
                w_wait(0, 2, (5,))

    @pl.when(outer)
    def _():
        w_wait(0, 7, (4,))
        w_start(2, 0)
        for piece in wholes:
            w_copy(2, 0, piece).wait_send()
        w_start(1, 0)
        w_start(1, 7)
        w_wait(1, 7, (4,))

    @pl.when(inner)
    def _():
        w_start(2, 2)

    slot_rows = [
        pl.multiple_of((owner - 4 * upper) * rows, 16) for owner in (me, partner)
    ]
    other_rows = [
        pl.multiple_of((owner - 4 * upper) * rows, 16)
        for owner in (beside, partner_of(beside))
    ]

    def rows_copy(slot):
        block = conv_rows.at[pl.ds(pl.multiple_of(slot_rows[slot] + margin, 16), rows), :]
        return remote(block, block, rows_send.at[slot], rows_recv.at[slot], beside)

    def edge_copy(turn):
        source = pl.multiple_of((1 - upper) * span + upper * margin, 16)
        target = pl.multiple_of(upper * (span + margin), 16)
        return remote(
            conv_rows.at[pl.ds(source, margin), :],
            conv_rows.at[pl.ds(target, margin), :],
            edge_send.at[turn],
            edge_recv,
            facing if turn == 0 else facing + 1 - 2 * odd,
        )

    lends = inner & (odd + upper == 1)
    reach = KERNEL // 2

    def gate(piece):
        for at in range(0, span + 2 * margin, (span + 2 * margin) // 2):
            block = slice(at, at + (span + 2 * margin) // 2)
            value = jnp.dot(
                conv_rows[block, :], half_b_ref[piece], preferred_element_type=jnp.float32
            )
            gates = jnp.dot(
                conv_rows[block, :], half_b_ref[2 + piece], preferred_element_type=jnp.float32
            )
            glu = (value * jax.nn.sigmoid(gates)).astype(jnp.bfloat16)
            padded[block, :] = glu.astype(jnp.float32)

    def columns_of(piece, side, at):
        return pl.ds(pl.multiple_of(piece * (2 * part) + side * part + at, 128), 128)

    def taps_of(piece, at):
        cols = columns_of(piece, odd, at)
        block = taps[:, cols]
        size = rows // 2
        for first in range(0, span, size):
            own = near[reach % 8, first + reach // 8 * 8 : first + reach // 8 * 8 + size, :]
            summed = jnp.zeros((size, 128), jnp.float32)
            for shift in range(8):
                start = first + margin - reach + shift
                ahead = padded[start : start + size + 24, at : at + 128]
                for skip in range(0, 32, 8):
                    offset = skip + shift
                    if offset < KERNEL:
                        term = ahead[skip : skip + size] * block[offset : offset + 1]
                        keep = near[shift, first + skip : first + skip + size, :] == own
                        summed = summed + jnp.where(keep, term, 0.0)
            depthwise[first : first + size, cols] = summed

    def deep_copy(order, at):
        turn = order * 2 + at // 128
        return remote(
            deep_out.at[turn], deep_in.at[turn], deep_send.at[turn], deep_recv.at[turn], beside
        )

    def piece_of(order):
        return upper if order == 0 else 1 - upper

    def convolve(order):
        piece = piece_of(order)
        gate(piece)
        for at in range(0, part, 128):
            taps_of(piece, at)
            cols = columns_of(piece, odd, at)
            for slot in range(2):
                deep_out[order * 2 + at // 128, slot * rows : (slot + 1) * rows, :] = depthwise[
                    pl.ds(other_rows[slot], rows), cols
                ].astype(jnp.bfloat16)
            deep_copy(order, at).start()

    def leave(turn, slot, owner):
        cols = pl.ds(pl.multiple_of(lax.div(owner, 2) * (2 * width), 128), 2 * width)
        return remote(
            leaving.at[pl.ds(slot * rows, rows), cols],
            handed_ref.at[:, cols],
            leave_send.at[turn, slot],
            leave_recv.at[turn],
            me if slot == 0 else partner,
            phase_next,
        )

    ends = (me, partner, facing, partner_of(facing))

    @pl.when(inner)
    def _():
        w_wait(0, 3, (6,))
        for away in range(1, shards):
            source = lax.rem(me + away, shards)
            remote(
                outbox.at[0],
                attended_ref.at[:, my_columns],
                out_send.at[0],
                out_recv.at[source],
                source,
            ).wait_recv()
        kept[0].wait()

        def output_part(owner):
            at = lax.div(owner, 2)
            cols = pl.ds(pl.multiple_of(at * (2 * width), 128), 2 * width)
            mixed = jnp.dot(attended_ref[...], full_a_ref[at], preferred_element_type=jnp.float32)
            for slot, source in enumerate((me, partner)):
                block = slice(slot * rows, (slot + 1) * rows)
                first = pl.ds(pl.multiple_of(source * rows, rows), rows)
                after[block, cols] = hidden[first, cols].astype(jnp.float32) + mixed[block]

        w_wait(0, 1)
        output_part(me)
        w_wait(0, 4)
        output_part(partner)
        w_wait(0, 5)
        output_part(facing)
        w_wait(0, 6)
        output_part(partner_of(facing))
        for slot in (0, 1):
            block = layer_norm(after[slot * rows : (slot + 1) * rows, :]).astype(jnp.bfloat16)
            at = pl.ds(pl.multiple_of(slot_rows[slot] + margin, 16), rows)
            conv_rows[at, :] = block
            if slot == 0:

                @pl.when(lends)
                def _():
                    for turn in range(2):
                        edge_copy(turn).start()

            rows_copy(slot).start()
        w_wait(2, 0, (3,))
        w_start(1, 2)
        w_wait(1, 0, (3,))
        kept[2].wait()
        w_wait(2, 2)
        edge_copy(0).wait_recv()
        for slot in range(2):
            rows_copy(slot).wait_recv()
        w_wait(1, 2, (5,))
        convolve(0)
        w_wait(1, 3, (6,))
        w_wait(2, 3)
        convolve(1)
        for order in range(2):
            for at in range(0, part, 128):
                deep_copy(order, at).wait_recv()
                cols = columns_of(piece_of(order), 1 - odd, at)
                for slot in range(2):
                    depthwise[pl.ds(slot_rows[slot], rows), cols] = deep_in[
                        order * 2 + at // 128, slot * rows : (slot + 1) * rows, :
                    ].astype(jnp.float32)
        kept[1].wait()
        for slot in (1, 0):
            block = layer_norm(depthwise[pl.ds(slot_rows[slot], rows), :])
            act = (block * jax.nn.sigmoid(block)).astype(jnp.bfloat16)
            at_rows = slice(slot * rows, (slot + 1) * rows)
            for turn, owner in enumerate(ends):
                if slot == 1:
                    w_wait(1, (1, 4, 5, 6)[turn])
                at = lax.div(owner, 2)
                cols = pl.ds(pl.multiple_of(at * (2 * width), 128), 2 * width)
                leaving[at_rows, cols] = (
                    after[at_rows, cols]
                    + jnp.dot(act, full_c_ref[at], preferred_element_type=jnp.float32)
                ).astype(jnp.bfloat16)
                leave(turn, slot, owner).start()

    for step in range(steps):
        for way, piece in hops(step):
            hop(step, way, piece).wait_send()
    for turn in range(turns - 1):
        out_copy(turn, target_of(turn)).wait_send()

    @pl.when(outer)
    def _():
        for copy in kept:
            copy.wait()
        out_copy(turns - 1, partner).wait_send()
        for load, kinds in ((0, (0, 4, 7)), (1, (0, 4, 7))):
            for kind in kinds:
                for piece in wholes:
                    w_copy(load, kind, piece).wait_send()

    @pl.when(inner)
    def _():
        for load, kinds in ((0, (1, 2, 3, 5, 6)), (1, (1, 2, 3, 5, 6)), (2, (2, 3))):
            for kind in kinds:
                for piece in wholes:
                    w_copy(load, kind, piece).wait_send()
        for slot in range(2):
            rows_copy(slot).wait_send()
        for order in range(2):
            for at in range(0, part, 128):
                deep_copy(order, at).wait_send()
        for turn, owner in enumerate(ends):
            for slot in range(2):
                leave(turn, slot, owner).wait_send()

    @pl.when(lends)
    def _():
        for turn in range(2):
            edge_copy(turn).wait_send()

    for turn, owner in enumerate(ends):
        leave(turn, 0, owner).wait_recv()


def block_call(shards, hidden, lengths, taps, weights):
    rows, depth = hidden.shape
    width = weights[0].shape[1]
    part = weights[4].shape[1]
    total = rows * shards
    steps = shards // 2
    margin = 16
    vmem = pl.BlockSpec(memory_space=pltpu.VMEM)
    smem = pl.BlockSpec(memory_space=pltpu.SMEM)
    anywhere = pl.BlockSpec(memory_space=pl.ANY)
    dma = pltpu.SemaphoreType.DMA
    bf16, f32 = jnp.bfloat16, jnp.float32
    return pl.pallas_call(
        functools.partial(block_kernel, shards, depth // HEADS),
        out_shape=jax.ShapeDtypeStruct((rows, depth), bf16),
        in_specs=[smem, anywhere, vmem] + [anywhere] * 6,
        out_specs=vmem,
        scratch_shapes=[
            pltpu.VMEM((total, depth), bf16),
            pltpu.VMEM((depth, 3 * width), bf16),
            pltpu.VMEM((shards // 2, depth, 2 * width), bf16),
            pltpu.VMEM((shards // 2, depth, part), bf16),
            pltpu.VMEM((shards // 2, depth, 2 * width), bf16),
            pltpu.VMEM((2 * rows, depth), bf16),
            pltpu.VMEM((2 * rows, depth), f32),
            pltpu.VMEM((total // 2 + 2 * margin, depth), bf16),
            pltpu.VMEM((8, total // 2 + 24, 128), jnp.int32),
            pltpu.VMEM(taps.shape, f32),
            pltpu.VMEM((total // 2 + 2 * margin, part), f32),
            pltpu.VMEM((total // 2, depth), f32),
            pltpu.VMEM((4, 2 * rows, 128), bf16),
            pltpu.VMEM((4, 2 * rows, 128), bf16),
            pltpu.VMEM((2 * rows, depth), bf16),
            pltpu.VMEM((total, width), bf16),
            pltpu.VMEM((total, width), bf16),
            pltpu.VMEM((total, width), bf16),
            pltpu.VMEM((steps, 2 * rows, width), bf16),
            dma((2 * steps, 2)),
            dma((2 * steps, 2)),
            dma((3,)),
            dma((steps,)),
            dma((shards,)),
            dma((4,)),
            dma((3, 8, 2)),
            dma((3, 8, 2)),
            dma((2,)),
            dma((2,)),
            dma((2,)),
            dma,
            dma((4,)),
            dma((4,)),
            dma((steps, 2)),
            dma((steps,)),
        ],
        compiler_params=pltpu.CompilerParams(
            collective_id=0, has_side_effects=True, vmem_limit_bytes=56 * 1024 * 1024
        ),
    )(lengths, hidden, taps, *weights)


def attention_general(hidden, utt_lengths, w_query, w_key, w_value, w_output, conv_in, conv_out):
    shards = lax.axis_size("seq")
    my_index = lax.axis_index("seq")
    local_rows = hidden.shape[0]
    width = hidden.shape[1]
    total_rows = local_rows * shards
    head_size = width // HEADS
    scale = 1.0 / math.sqrt(head_size)
    groups = min(HEADS, shards)
    group_heads = HEADS // groups
    parts = shards // groups
    part_rows = local_rows // parts
    group_width = group_heads * head_size
    full_query, full_key, full_value, full_output, full_conv_in, full_conv_out = (
        lax.all_gather(w_query, "seq", axis=1, tiled=True),
        lax.all_gather(w_key, "seq", axis=1, tiled=True),
        lax.all_gather(w_value, "seq", axis=1, tiled=True),
        lax.all_gather(w_output, "seq", axis=1, tiled=True),
        lax.all_gather(conv_in, "seq", axis=1, tiled=True),
        lax.all_gather(conv_out, "seq", axis=1, tiled=True),
    )
    normed = layer_norm(hidden.astype(jnp.float32)).astype(jnp.bfloat16)
    query = jnp.dot(normed, full_query, preferred_element_type=jnp.float32).astype(jnp.bfloat16)
    key_proj = jnp.dot(normed, full_key, preferred_element_type=jnp.float32).astype(jnp.bfloat16)
    value_proj = jnp.dot(normed, full_value, preferred_element_type=jnp.float32).astype(
        jnp.bfloat16
    )
    shaped = query.reshape(parts, part_rows, groups, group_width).transpose(2, 0, 1, 3)
    query_pieces = shaped.reshape(shards, part_rows, group_width)
    kv_local = jnp.concatenate(
        [
            key_proj.reshape(local_rows, groups, group_width),
            value_proj.reshape(local_rows, groups, group_width),
        ],
        axis=2,
    )
    copies = jnp.broadcast_to(
        kv_local.transpose(1, 0, 2)[:, None], (groups, parts, local_rows, 2 * group_width)
    )
    copies = copies.reshape(shards, local_rows, 2 * group_width)
    query_got, kv_got = (
        lax.all_to_all(query_pieces, "seq", split_axis=0, concat_axis=0, tiled=True),
        lax.all_to_all(copies, "seq", split_axis=0, concat_axis=0, tiled=True),
    )
    key_value = kv_got.reshape(total_rows, 2 * group_width)
    count = shards * part_rows
    my_part = my_index % parts
    row_ids = jnp.arange(count, dtype=jnp.int32)
    query_pos = row_ids // part_rows * local_rows + my_part * part_rows + row_ids % part_rows
    queries = query_got.reshape(count, group_heads, head_size)
    key_rows = key_value[:, :group_width].reshape(total_rows, group_heads, head_size)
    value_rows = key_value[:, group_width:].reshape(total_rows, group_heads, head_size)
    seg_all = segment_ids(jnp.arange(total_rows, dtype=jnp.int32), utt_lengths)
    seg_query = segment_ids(query_pos, utt_lengths)
    query_block = math.gcd(512, count)
    blocks = count // query_block

    def attend_block(operands):
        block_query, block_seg = operands
        scores = (
            jnp.einsum("qhd,khd->hqk", block_query, key_rows, preferred_element_type=jnp.float32)
            * scale
        )
        allowed = (block_seg[:, None] == seg_all[None, :])[None]
        scores = jnp.where(allowed, scores, -1e30)
        peak = jnp.max(scores, axis=2, keepdims=True)
        expw = jnp.where(allowed, jnp.exp(scores - peak), 0.0)
        total_weight = jnp.sum(expw, axis=2)
        mixed = jnp.einsum(
            "hqk,khd->hqd",
            expw.astype(jnp.bfloat16),
            value_rows,
            preferred_element_type=jnp.float32,
        )
        mixed = mixed / total_weight[:, :, None]
        return mixed.transpose(1, 0, 2).astype(jnp.bfloat16)

    attended = lax.map(
        attend_block,
        (
            queries.reshape(blocks, query_block, group_heads, head_size),
            seg_query.reshape(blocks, query_block),
        ),
    )
    outgoing = attended.reshape(shards, part_rows, group_width)
    returned = lax.all_to_all(outgoing, "seq", split_axis=0, concat_axis=0, tiled=True)
    attended_local = (
        returned.reshape(groups, parts, part_rows, group_width)
        .transpose(1, 2, 0, 3)
        .reshape(local_rows, width)
    )
    return attended_local, full_output, full_conv_in, full_conv_out


def body(frames, lengths, w_query, w_key, w_value, w_output, conv_in, conv_taps, conv_out):
    hidden = frames[0]
    utt_lengths = lengths[0]
    shards = lax.axis_size("seq")
    my_index = lax.axis_index("seq")
    local_rows = hidden.shape[0]
    width = hidden.shape[1]
    total_rows = local_rows * shards
    phases = lax.axis_size("phase")
    if phases > 2 and shards == 8 and width // shards == 128 and local_rows % 32 == 0:
        weights = (w_query[0], w_key[0], w_value[0], w_output[0], conv_in[0], conv_out[0])
        return block_call(shards, hidden, utt_lengths, conv_taps[0], weights)[None]
    attended_local, full_output, full_conv_in, full_conv_out = attention_general(
        hidden, utt_lengths, w_query[0], w_key[0], w_value[0], w_output[0], conv_in[0], conv_out[0]
    )
    after_attn = hidden.astype(jnp.float32) + jnp.dot(
        attended_local, full_output, preferred_element_type=jnp.float32
    )
    conv_normed = layer_norm(after_attn).astype(jnp.bfloat16)
    gates = jnp.dot(conv_normed, full_conv_in, preferred_element_type=jnp.float32)
    glu = (gates[:, :width] * jax.nn.sigmoid(gates[:, width:])).astype(jnp.bfloat16)
    reach = KERNEL // 2
    padded = padded_2(glu, (("seq", 0),), KERNEL // 2)
    padded_pos = my_index * local_rows - reach + jnp.arange(local_rows + 2 * reach, dtype=jnp.int32)
    inside = (padded_pos >= 0) & (padded_pos < total_rows)
    padded_seg = jnp.where(inside, segment_ids(padded_pos, utt_lengths), -1)
    own_seg = padded_seg[reach : reach + local_rows]
    taps = conv_taps[0]
    depthwise = jnp.zeros((local_rows, width), jnp.float32)
    for offset in range(KERNEL):
        keep = padded_seg[offset : offset + local_rows] == own_seg
        term = padded[offset : offset + local_rows].astype(jnp.float32) * taps[offset].astype(
            jnp.float32
        )
        depthwise = depthwise + jnp.where(keep[:, None], term, 0.0)
    conv_act = layer_norm(depthwise)
    conv_act = (conv_act * jax.nn.sigmoid(conv_act)).astype(jnp.bfloat16)
    block_out = (
        after_attn + jnp.dot(conv_act, full_conv_out, preferred_element_type=jnp.float32)
    ).astype(jnp.bfloat16)
    passed = passed_along(block_out, "phase", 1)
    return passed[None]


def solution(mesh):
    in_specs = (
        P("phase", "seq", None),
        P("phase", None),
        P("phase", None, "seq"),
        P("phase", None, "seq"),
        P("phase", None, "seq"),
        P("phase", None, "seq"),
        P("phase", None, "seq"),
        P("phase", None, None),
        P("phase", None, "seq"),
    )
    out_specs = P("phase", "seq", None)
    return jax.shard_map(body, mesh=mesh, in_specs=in_specs, out_specs=out_specs, check_vma=False)
```

```python
import functools
import math

import jax
import jax.numpy as jnp
from jax import lax
from jax.experimental import pallas as pl
from jax.experimental.pallas import tpu as pltpu
from jax.sharding import PartitionSpec as P

HEADS = 16
KERNEL = 31
MESH = pl.DeviceIdType.MESH


def padded_2(block, sides, width):
    for axis, dim in sides:
        count = lax.axis_size(axis)
        forward = [(i, i + 1) for i in range(count - 1)]
        backward = [(target, source) for source, target in forward]
        low = lax.ppermute(
            lax.slice_in_dim(block, block.shape[dim] - width, None, axis=dim), axis, forward
        )
        high = lax.ppermute(lax.slice_in_dim(block, 0, width, axis=dim), axis, backward)
        block = jnp.concatenate([low, block, high], axis=dim)
    return block


def passed_along(block, axis, distance):
    devices = range(lax.axis_size(axis))
    route = [((i - distance) % len(devices), i) for i in devices]
    return lax.ppermute(block, axis, route)


def layer_norm(values):
    centre = values - jnp.mean(values, axis=-1, keepdims=True)
    spread = jnp.mean(centre * centre, axis=-1, keepdims=True)
    return centre * lax.rsqrt(spread + 1e-05)


def segment_ids(positions, lengths):
    order = jnp.arange(lengths.shape[0], dtype=jnp.int32)
    bounds = jnp.sum(jnp.where(order[None, :] <= order[:, None], lengths[None, :], 0), axis=1)
    return jnp.sum((positions[:, None] >= bounds[None, :]).astype(jnp.int32), axis=1)


def ring_index(place, shards):
    place = lax.rem(place + shards, shards)
    late = lax.div(place, shards // 2)
    return (1 - late) * (2 * place) + late * (2 * (shards - 1 - place) + 1)


def segment_of(positions, bounds):
    segment = jnp.zeros(positions.shape, jnp.int32)
    for bound in bounds:
        segment = segment + (positions >= bound).astype(jnp.int32)
    return segment


def block_kernel(
    shards,
    head_size,
    lengths_ref,
    frames_ref,
    taps_ref,
    query_ref,
    key_ref,
    value_ref,
    w_a_ref,
    w_b_ref,
    w_c_ref,
    handed_ref,
    hidden,
    qkv,
    full_a_ref,
    half_b_ref,
    full_c_ref,
    attended_ref,
    after,
    conv_rows,
    near,
    taps,
    padded,
    depthwise,
    deep_out,
    deep_in,
    leaving,
    query,
    keys,
    values,
    outbox,
    send_sem,
    recv_sem,
    own_sem,
    out_send,
    out_recv,
    in_sem,
    w_send,
    w_recv,
    rows_send,
    rows_recv,
    edge_send,
    edge_recv,
    deep_send,
    deep_recv,
    leave_send,
    leave_recv,
):
    rows = frames_ref.shape[0]
    depth = frames_ref.shape[1]
    width = query_ref.shape[1]
    part = w_b_ref.shape[1]
    me = lax.axis_index("seq")
    own_rows = pl.ds(pl.multiple_of(me * rows, rows), rows)
    loads_in = [pltpu.make_async_copy(frames_ref, hidden.at[own_rows, :], in_sem.at[3])]
    for i, ref in enumerate((query_ref, key_ref, value_ref)):
        loads_in.append(
            pltpu.make_async_copy(ref, qkv.at[:, pl.ds(i * width, width)], in_sem.at[i])
        )
    for copy in loads_in:
        copy.start()
    steps = shards // 2
    odd = lax.rem(me, 2)
    place = (1 - odd) * lax.div(me, 2) + odd * (shards - 1 - lax.div(me, 2))
    right, left = ring_index(place + 1, shards), ring_index(place - 1, shards)
    half = lax.rem(lax.div(me, 2), 2)
    upper = lax.div(me, 4)

    def partner_of(owner):
        return owner + 2 - 4 * lax.rem(lax.div(owner, 2), 2)

    def inner_of(owner):
        return lax.rem(lax.div(lax.div(owner, 2) + 1, 2), 2)

    beside = me + 1 - 2 * odd
    facing = me + 2 - 4 * upper
    partner = partner_of(me)
    inner = inner_of(me) == 1
    outer = inner_of(me) == 0
    home = inner_of(me) * me + (1 - inner_of(me)) * partner

    barrier = pltpu.get_barrier_semaphore()
    for away in range(1, shards):
        peer = lax.rem(me + away, shards)
        pl.semaphore_signal(barrier, inc=1, device_id={"seq": peer}, device_id_type=MESH)
    phase = lax.axis_index("phase")
    phases = lax.axis_size("phase")
    phase_next = lax.rem(phase + 1, phases)
    phase_back = lax.rem(phase + phases - 1, phases)
    for other in (phase_next, phase_back):
        for peer in (me, partner):
            pl.semaphore_signal(
                barrier, inc=1, device_id={"phase": other, "seq": peer}, device_id_type=MESH
            )

    loads_in[0].wait()
    pl.semaphore_wait(barrier, shards + 3)

    def remote(source, target, sent, got, peer, onward=None):
        place_of = {"seq": peer} if onward is None else {"phase": onward, "seq": peer}
        return pltpu.make_async_remote_copy(
            src_ref=source,
            dst_ref=target,
            send_sem=sent,
            recv_sem=got,
            device_id=place_of,
            device_id_type=MESH,
        )

    def hop(step, way, piece):
        owner = ring_index(place - step if way == 0 else place + step, shards)
        size = rows // 2
        block = hidden.at[pl.ds(pl.multiple_of(owner * rows + piece * size, 16), size), :]
        at = step * 2 + way
        peer = right if way == 0 else left
        return remote(block, block, send_sem.at[at, piece], recv_sem.at[at, piece], peer)

    def hops(step):
        pairs = [(way, piece) for piece in range(2) for way in range(2)]
        return [(way, piece) for way, piece in pairs if step < steps - 1 or way == piece]

    def forward(step):
        onward = hops(step + 1) if step < steps - 1 else ()
        for way, piece in hops(step):
            hop(step, way, piece).wait_recv()
            if (way, piece) in onward:
                hop(step + 1, way, piece).start()

    def project(owner):
        at = pl.ds(pl.multiple_of(owner * rows, rows), rows)
        block = layer_norm(hidden[at, :].astype(jnp.float32)).astype(jnp.bfloat16)
        both = jnp.dot(block, qkv[...], preferred_element_type=jnp.float32).astype(jnp.bfloat16)
        query[at, :] = both[:, :width] * jnp.bfloat16(1.0 / math.sqrt(head_size))
        keys[at, :] = both[:, width : 2 * width]
        values[at, :] = both[:, 2 * width :]

    fulls = ((w_a_ref, full_a_ref), (w_c_ref, full_c_ref), (w_b_ref, half_b_ref))
    wholes = range(2)

    def chunk(load, owner, first, size):
        full = fulls[load][1]
        if load == 2:
            return full.at[lax.div(owner, 2), pl.ds(first, size), :]
        cols = pl.ds(pl.multiple_of(lax.rem(owner, 2) * width, 128), width)
        return full.at[lax.div(owner, 2), pl.ds(first, size), cols]

    def w_copy(load, kind, piece):
        own = fulls[load][0]
        size = depth // 2
        owner = (me, me, me, partner, beside, facing, partner_of(facing), me)[kind]
        peer = (partner, beside, facing, facing, partner, beside, beside, beside)[kind]
        target = chunk(load, owner, piece * size, size)
        source = own.at[pl.ds(piece * size, size), :] if kind in (0, 1, 2, 7) else target
        return remote(
            source, target, w_send.at[load, kind, piece], w_recv.at[load, kind, piece], peer
        )

    def w_start(load, kind):
        for piece in wholes:
            w_copy(load, kind, piece).start()

    def w_wait(load, kind, then=()):
        for piece in wholes:
            w_copy(load, kind, piece).wait_recv()
            for more in then:
                w_copy(load, more, piece).start()

    for way, piece in hops(0):
        hop(0, way, piece).start()

    @pl.when(inner)
    def _():
        w_start(0, 1)
        w_start(1, 1)

    kept = [
        pltpu.make_async_copy(fulls[load][0], chunk(load, me, 0, depth), own_sem.at[load])
        for load in range(3)
    ]
    for copy in kept:
        copy.start()
    bounds = [lengths_ref[0]]
    for utt in range(1, lengths_ref.shape[0]):
        bounds.append(bounds[-1] + lengths_ref[utt])
    seg_col = segment_of(lax.broadcasted_iota(jnp.int32, (1, rows * shards), 1), bounds)
    margin = 16
    span = rows * steps
    first_row = upper * span
    for shift in range(near.shape[0]):
        positions = lax.broadcasted_iota(jnp.int32, near.shape[1:], 0)
        positions = positions + (first_row + shift - KERNEL // 2)
        near[shift] = jnp.where(positions >= 0, segment_of(positions, bounds), -1)
    outside = pl.multiple_of(upper * (span + margin), 16)
    conv_rows[pl.ds(outside, margin), :] = jnp.zeros((margin, depth), jnp.bfloat16)
    taps[...] = taps_ref[...].astype(jnp.float32)

    for copy in loads_in[1:]:
        copy.wait()
    project(me)
    for step in range(steps):
        forward(step)
        if step == steps - 2:

            @pl.when(outer)
            def _():
                w_start(0, 0)
                w_start(0, 7)

            @pl.when(inner)
            def _():
                w_start(0, 2)

        project(ring_index(place - 1 - step, shards))
        if step < steps - 1:
            project(ring_index(place + 1 + step, shards))

    lane = lax.broadcasted_iota(jnp.int32, (rows, width), 1)
    my_columns = pl.ds(pl.multiple_of(me * width, 128), width)

    def attend(owner):
        at = pl.ds(pl.multiple_of(owner * rows, rows), rows)
        block = query[at, :]
        positions = lax.broadcasted_iota(jnp.int32, (rows, 1), 0) + owner * rows
        allowed = segment_of(positions, bounds) == seg_col
        result = jnp.zeros((rows, width), jnp.float32)
        for head in range(width // head_size):
            mine = (lane >= head * head_size) & (lane < (head + 1) * head_size)
            scores = lax.dot_general(
                jnp.where(mine, block, jnp.bfloat16(0)),
                keys[...],
                (((1,), (1,)), ((), ())),
                preferred_element_type=jnp.float32,
            )
            scores = jnp.where(allowed, scores, -1e30)
            peak = jnp.max(scores, axis=1, keepdims=True)
            expw = jnp.exp(scores - peak)
            total = jnp.sum(expw, axis=1, keepdims=True)
            mixed = jnp.dot(
                expw.astype(jnp.bfloat16), values[...], preferred_element_type=jnp.float32
            )
            result = jnp.where(mine, mixed / total, result)
        return result.astype(jnp.bfloat16)

    def out_copy(turn, target):
        return remote(
            outbox.at[turn],
            attended_ref.at[:, my_columns],
            out_send.at[turn],
            out_recv.at[me],
            target,
        )

    turns = steps

    def target_of(turn):
        return 2 + lax.rem(home - 2 + 1 + turn, turns)

    for turn in range(turns):
        target = target_of(turn)
        outbox[turn, :rows, :] = attend(target)
        outbox[turn, rows:, :] = attend(partner_of(target))
        if turn < turns - 1:
            out_copy(turn, target).start()
        else:

            @pl.when(outer)
            def _():
                out_copy(turns - 1, partner).start()

            @pl.when(inner)
            def _():
                attended_ref[:, my_columns] = outbox[turns - 1]

        if turn == 2:

            @pl.when(inner)
            def _():
                w_wait(0, 0, (3,))
                w_wait(0, 2, (5,))

    @pl.when(outer)
    def _():
        w_wait(0, 7, (4,))
        w_start(2, 0)
        for piece in wholes:
            w_copy(2, 0, piece).wait_send()
        w_start(1, 0)
        w_start(1, 7)
        w_wait(1, 7, (4,))

    @pl.when(inner)
    def _():
        w_start(2, 2)

    slot_rows = [
        pl.multiple_of((owner - 4 * upper) * rows, 16) for owner in (me, partner)
    ]
    other_rows = [
        pl.multiple_of((owner - 4 * upper) * rows, 16)
        for owner in (beside, partner_of(beside))
    ]

    def rows_copy(slot):
        block = conv_rows.at[pl.ds(pl.multiple_of(slot_rows[slot] + margin, 16), rows), :]
        return remote(block, block, rows_send.at[slot], rows_recv.at[slot], beside)

    def edge_copy(turn):
        source = pl.multiple_of((1 - upper) * span + upper * margin, 16)
        target = pl.multiple_of(upper * (span + margin), 16)
        return remote(
            conv_rows.at[pl.ds(source, margin), :],
            conv_rows.at[pl.ds(target, margin), :],
            edge_send.at[turn],
            edge_recv,
            facing if turn == 0 else facing + 1 - 2 * odd,
        )

    lends = inner & (odd + upper == 1)
    reach = KERNEL // 2

    def gate(piece):
        for at in range(0, span + 2 * margin, (span + 2 * margin) // 2):
            block = slice(at, at + (span + 2 * margin) // 2)
            value = jnp.dot(
                conv_rows[block, :], half_b_ref[piece], preferred_element_type=jnp.float32
            )
            gates = jnp.dot(
                conv_rows[block, :], half_b_ref[2 + piece], preferred_element_type=jnp.float32
            )
            glu = (value * jax.nn.sigmoid(gates)).astype(jnp.bfloat16)
            padded[block, :] = glu.astype(jnp.float32)

    def columns_of(piece, side, at):
        return pl.ds(pl.multiple_of(piece * (2 * part) + side * part + at, 128), 128)

    def taps_of(piece, at):
        cols = columns_of(piece, odd, at)
        block = taps[:, cols]
        size = rows // 2
        for first in range(0, span, size):
            own = near[reach % 8, first + reach // 8 * 8 : first + reach // 8 * 8 + size, :]
            summed = jnp.zeros((size, 128), jnp.float32)
            for shift in range(8):
                start = first + margin - reach + shift
                ahead = padded[start : start + size + 24, at : at + 128]
                for skip in range(0, 32, 8):
                    offset = skip + shift
                    if offset < KERNEL:
                        term = ahead[skip : skip + size] * block[offset : offset + 1]
                        keep = near[shift, first + skip : first + skip + size, :] == own
                        summed = summed + jnp.where(keep, term, 0.0)
            depthwise[first : first + size, cols] = summed

    def deep_copy(order, at):
        turn = order * 2 + at // 128
        return remote(
            deep_out.at[turn], deep_in.at[turn], deep_send.at[turn], deep_recv.at[turn], beside
        )

    def piece_of(order):
        return upper if order == 0 else 1 - upper

    def convolve(order):
        piece = piece_of(order)
        gate(piece)
        for at in range(0, part, 128):
            taps_of(piece, at)
            cols = columns_of(piece, odd, at)
            for slot in range(2):
                deep_out[order * 2 + at // 128, slot * rows : (slot + 1) * rows, :] = depthwise[
                    pl.ds(other_rows[slot], rows), cols
                ].astype(jnp.bfloat16)
            deep_copy(order, at).start()

    def leave(turn, slot, owner):
        cols = pl.ds(pl.multiple_of(lax.div(owner, 2) * (2 * width), 128), 2 * width)
        return remote(
            leaving.at[pl.ds(slot * rows, rows), cols],
            handed_ref.at[:, cols],
            leave_send.at[turn, slot],
            leave_recv.at[turn],
            me if slot == 0 else partner,
            phase_next,
        )

    ends = (me, partner, facing, partner_of(facing))

    @pl.when(inner)
    def _():
        w_wait(0, 3, (6,))
        for away in range(1, shards):
            source = lax.rem(me + away, shards)
            remote(
                outbox.at[0],
                attended_ref.at[:, my_columns],
                out_send.at[0],
                out_recv.at[source],
                source,
            ).wait_recv()
        kept[0].wait()

        def output_part(owner):
            at = lax.div(owner, 2)
            cols = pl.ds(pl.multiple_of(at * (2 * width), 128), 2 * width)
            mixed = jnp.dot(attended_ref[...], full_a_ref[at], preferred_element_type=jnp.float32)
            for slot, source in enumerate((me, partner)):
                block = slice(slot * rows, (slot + 1) * rows)
                first = pl.ds(pl.multiple_of(source * rows, rows), rows)
                after[block, cols] = hidden[first, cols].astype(jnp.float32) + mixed[block]

        w_wait(0, 1)
        output_part(me)
        w_wait(0, 4)
        output_part(partner)
        w_wait(0, 5)
        output_part(facing)
        w_wait(0, 6)
        output_part(partner_of(facing))
        for slot in (0, 1):
            block = layer_norm(after[slot * rows : (slot + 1) * rows, :]).astype(jnp.bfloat16)
            at = pl.ds(pl.multiple_of(slot_rows[slot] + margin, 16), rows)
            conv_rows[at, :] = block
            if slot == 0:

                @pl.when(lends)
                def _():
                    for turn in range(2):
                        edge_copy(turn).start()

            rows_copy(slot).start()
        w_wait(2, 0, (3,))
        kept[2].wait()
        w_wait(2, 2)
        edge_copy(0).wait_recv()
        for slot in range(2):
            rows_copy(slot).wait_recv()
        w_start(1, 2)
        w_wait(1, 0, (3,))
        convolve(0)
        w_wait(1, 2, (5,))
        w_wait(1, 3, (6,))
        w_wait(2, 3)
        convolve(1)
        for order in range(2):
            for at in range(0, part, 128):
                deep_copy(order, at).wait_recv()
                cols = columns_of(piece_of(order), 1 - odd, at)
                for slot in range(2):
                    depthwise[pl.ds(slot_rows[slot], rows), cols] = deep_in[
                        order * 2 + at // 128, slot * rows : (slot + 1) * rows, :
                    ].astype(jnp.float32)
        kept[1].wait()
        for slot in (1, 0):
            block = layer_norm(depthwise[pl.ds(slot_rows[slot], rows), :])
            act = (block * jax.nn.sigmoid(block)).astype(jnp.bfloat16)
            at_rows = slice(slot * rows, (slot + 1) * rows)
            for turn, owner in enumerate(ends):
                if slot == 1:
                    w_wait(1, (1, 4, 5, 6)[turn])
                at = lax.div(owner, 2)
                cols = pl.ds(pl.multiple_of(at * (2 * width), 128), 2 * width)
                leaving[at_rows, cols] = (
                    after[at_rows, cols]
                    + jnp.dot(act, full_c_ref[at], preferred_element_type=jnp.float32)
                ).astype(jnp.bfloat16)
                leave(turn, slot, owner).start()

    for step in range(steps):
        for way, piece in hops(step):
            hop(step, way, piece).wait_send()
    for turn in range(turns - 1):
        out_copy(turn, target_of(turn)).wait_send()

    @pl.when(outer)
    def _():
        for copy in kept:
            copy.wait()
        out_copy(turns - 1, partner).wait_send()
        for load, kinds in ((0, (0, 4, 7)), (1, (0, 4, 7))):
            for kind in kinds:
                for piece in wholes:
                    w_copy(load, kind, piece).wait_send()

    @pl.when(inner)
    def _():
        for load, kinds in ((0, (1, 2, 3, 5, 6)), (1, (1, 2, 3, 5, 6)), (2, (2, 3))):
            for kind in kinds:
                for piece in wholes:
                    w_copy(load, kind, piece).wait_send()
        for slot in range(2):
            rows_copy(slot).wait_send()
        for order in range(2):
            for at in range(0, part, 128):
                deep_copy(order, at).wait_send()
        for turn, owner in enumerate(ends):
            for slot in range(2):
                leave(turn, slot, owner).wait_send()

    @pl.when(lends)
    def _():
        for turn in range(2):
            edge_copy(turn).wait_send()

    for turn, owner in enumerate(ends):
        leave(turn, 0, owner).wait_recv()


def block_call(shards, hidden, lengths, taps, weights):
    rows, depth = hidden.shape
    width = weights[0].shape[1]
    part = weights[4].shape[1]
    total = rows * shards
    steps = shards // 2
    margin = 16
    vmem = pl.BlockSpec(memory_space=pltpu.VMEM)
    smem = pl.BlockSpec(memory_space=pltpu.SMEM)
    anywhere = pl.BlockSpec(memory_space=pl.ANY)
    dma = pltpu.SemaphoreType.DMA
    bf16, f32 = jnp.bfloat16, jnp.float32
    return pl.pallas_call(
        functools.partial(block_kernel, shards, depth // HEADS),
        out_shape=jax.ShapeDtypeStruct((rows, depth), bf16),
        in_specs=[smem, anywhere, vmem] + [anywhere] * 6,
        out_specs=vmem,
        scratch_shapes=[
            pltpu.VMEM((total, depth), bf16),
            pltpu.VMEM((depth, 3 * width), bf16),
            pltpu.VMEM((shards // 2, depth, 2 * width), bf16),
            pltpu.VMEM((shards // 2, depth, part), bf16),
            pltpu.VMEM((shards // 2, depth, 2 * width), bf16),
            pltpu.VMEM((2 * rows, depth), bf16),
            pltpu.VMEM((2 * rows, depth), f32),
            pltpu.VMEM((total // 2 + 2 * margin, depth), bf16),
            pltpu.VMEM((8, total // 2 + 24, 128), jnp.int32),
            pltpu.VMEM(taps.shape, f32),
            pltpu.VMEM((total // 2 + 2 * margin, part), f32),
            pltpu.VMEM((total // 2, depth), f32),
            pltpu.VMEM((4, 2 * rows, 128), bf16),
            pltpu.VMEM((4, 2 * rows, 128), bf16),
            pltpu.VMEM((2 * rows, depth), bf16),
            pltpu.VMEM((total, width), bf16),
            pltpu.VMEM((total, width), bf16),
            pltpu.VMEM((total, width), bf16),
            pltpu.VMEM((steps, 2 * rows, width), bf16),
            dma((2 * steps, 2)),
            dma((2 * steps, 2)),
            dma((3,)),
            dma((steps,)),
            dma((shards,)),
            dma((4,)),
            dma((3, 8, 2)),
            dma((3, 8, 2)),
            dma((2,)),
            dma((2,)),
            dma((2,)),
            dma,
            dma((4,)),
            dma((4,)),
            dma((steps, 2)),
            dma((steps,)),
        ],
        compiler_params=pltpu.CompilerParams(
            collective_id=0, has_side_effects=True, vmem_limit_bytes=56 * 1024 * 1024
        ),
    )(lengths, hidden, taps, *weights)


def attention_general(hidden, utt_lengths, w_query, w_key, w_value, w_output, conv_in, conv_out):
    shards = lax.axis_size("seq")
    my_index = lax.axis_index("seq")
    local_rows = hidden.shape[0]
    width = hidden.shape[1]
    total_rows = local_rows * shards
    head_size = width // HEADS
    scale = 1.0 / math.sqrt(head_size)
    groups = min(HEADS, shards)
    group_heads = HEADS // groups
    parts = shards // groups
    part_rows = local_rows // parts
    group_width = group_heads * head_size
    full_query, full_key, full_value, full_output, full_conv_in, full_conv_out = (
        lax.all_gather(w_query, "seq", axis=1, tiled=True),
        lax.all_gather(w_key, "seq", axis=1, tiled=True),
        lax.all_gather(w_value, "seq", axis=1, tiled=True),
        lax.all_gather(w_output, "seq", axis=1, tiled=True),
        lax.all_gather(conv_in, "seq", axis=1, tiled=True),
        lax.all_gather(conv_out, "seq", axis=1, tiled=True),
    )
    normed = layer_norm(hidden.astype(jnp.float32)).astype(jnp.bfloat16)
    query = jnp.dot(normed, full_query, preferred_element_type=jnp.float32).astype(jnp.bfloat16)
    key_proj = jnp.dot(normed, full_key, preferred_element_type=jnp.float32).astype(jnp.bfloat16)
    value_proj = jnp.dot(normed, full_value, preferred_element_type=jnp.float32).astype(
        jnp.bfloat16
    )
    shaped = query.reshape(parts, part_rows, groups, group_width).transpose(2, 0, 1, 3)
    query_pieces = shaped.reshape(shards, part_rows, group_width)
    kv_local = jnp.concatenate(
        [
            key_proj.reshape(local_rows, groups, group_width),
            value_proj.reshape(local_rows, groups, group_width),
        ],
        axis=2,
    )
    copies = jnp.broadcast_to(
        kv_local.transpose(1, 0, 2)[:, None], (groups, parts, local_rows, 2 * group_width)
    )
    copies = copies.reshape(shards, local_rows, 2 * group_width)
    query_got, kv_got = (
        lax.all_to_all(query_pieces, "seq", split_axis=0, concat_axis=0, tiled=True),
        lax.all_to_all(copies, "seq", split_axis=0, concat_axis=0, tiled=True),
    )
    key_value = kv_got.reshape(total_rows, 2 * group_width)
    count = shards * part_rows
    my_part = my_index % parts
    row_ids = jnp.arange(count, dtype=jnp.int32)
    query_pos = row_ids // part_rows * local_rows + my_part * part_rows + row_ids % part_rows
    queries = query_got.reshape(count, group_heads, head_size)
    key_rows = key_value[:, :group_width].reshape(total_rows, group_heads, head_size)
    value_rows = key_value[:, group_width:].reshape(total_rows, group_heads, head_size)
    seg_all = segment_ids(jnp.arange(total_rows, dtype=jnp.int32), utt_lengths)
    seg_query = segment_ids(query_pos, utt_lengths)
    query_block = math.gcd(512, count)
    blocks = count // query_block

    def attend_block(operands):
        block_query, block_seg = operands
        scores = (
            jnp.einsum("qhd,khd->hqk", block_query, key_rows, preferred_element_type=jnp.float32)
            * scale
        )
        allowed = (block_seg[:, None] == seg_all[None, :])[None]
        scores = jnp.where(allowed, scores, -1e30)
        peak = jnp.max(scores, axis=2, keepdims=True)
        expw = jnp.where(allowed, jnp.exp(scores - peak), 0.0)
        total_weight = jnp.sum(expw, axis=2)
        mixed = jnp.einsum(
            "hqk,khd->hqd",
            expw.astype(jnp.bfloat16),
            value_rows,
            preferred_element_type=jnp.float32,
        )
        mixed = mixed / total_weight[:, :, None]
        return mixed.transpose(1, 0, 2).astype(jnp.bfloat16)

    attended = lax.map(
        attend_block,
        (
            queries.reshape(blocks, query_block, group_heads, head_size),
            seg_query.reshape(blocks, query_block),
        ),
    )
    outgoing = attended.reshape(shards, part_rows, group_width)
    returned = lax.all_to_all(outgoing, "seq", split_axis=0, concat_axis=0, tiled=True)
    attended_local = (
        returned.reshape(groups, parts, part_rows, group_width)
        .transpose(1, 2, 0, 3)
        .reshape(local_rows, width)
    )
    return attended_local, full_output, full_conv_in, full_conv_out


def body(frames, lengths, w_query, w_key, w_value, w_output, conv_in, conv_taps, conv_out):
    hidden = frames[0]
    utt_lengths = lengths[0]
    shards = lax.axis_size("seq")
    my_index = lax.axis_index("seq")
    local_rows = hidden.shape[0]
    width = hidden.shape[1]
    total_rows = local_rows * shards
    phases = lax.axis_size("phase")
    if phases > 2 and shards == 8 and width // shards == 128 and local_rows % 32 == 0:
        weights = (w_query[0], w_key[0], w_value[0], w_output[0], conv_in[0], conv_out[0])
        return block_call(shards, hidden, utt_lengths, conv_taps[0], weights)[None]
    attended_local, full_output, full_conv_in, full_conv_out = attention_general(
        hidden, utt_lengths, w_query[0], w_key[0], w_value[0], w_output[0], conv_in[0], conv_out[0]
    )
    after_attn = hidden.astype(jnp.float32) + jnp.dot(
        attended_local, full_output, preferred_element_type=jnp.float32
    )
    conv_normed = layer_norm(after_attn).astype(jnp.bfloat16)
    gates = jnp.dot(conv_normed, full_conv_in, preferred_element_type=jnp.float32)
    glu = (gates[:, :width] * jax.nn.sigmoid(gates[:, width:])).astype(jnp.bfloat16)
    reach = KERNEL // 2
    padded = padded_2(glu, (("seq", 0),), KERNEL // 2)
    padded_pos = my_index * local_rows - reach + jnp.arange(local_rows + 2 * reach, dtype=jnp.int32)
    inside = (padded_pos >= 0) & (padded_pos < total_rows)
    padded_seg = jnp.where(inside, segment_ids(padded_pos, utt_lengths), -1)
    own_seg = padded_seg[reach : reach + local_rows]
    taps = conv_taps[0]
    depthwise = jnp.zeros((local_rows, width), jnp.float32)
    for offset in range(KERNEL):
        keep = padded_seg[offset : offset + local_rows] == own_seg
        term = padded[offset : offset + local_rows].astype(jnp.float32) * taps[offset].astype(
            jnp.float32
        )
        depthwise = depthwise + jnp.where(keep[:, None], term, 0.0)
    conv_act = layer_norm(depthwise)
    conv_act = (conv_act * jax.nn.sigmoid(conv_act)).astype(jnp.bfloat16)
    block_out = (
        after_attn + jnp.dot(conv_act, full_conv_out, preferred_element_type=jnp.float32)
    ).astype(jnp.bfloat16)
    passed = passed_along(block_out, "phase", 1)
    return passed[None]


def solution(mesh):
    in_specs = (
        P("phase", "seq", None),
        P("phase", None),
        P("phase", None, "seq"),
        P("phase", None, "seq"),
        P("phase", None, "seq"),
        P("phase", None, "seq"),
        P("phase", None, "seq"),
        P("phase", None, None),
        P("phase", None, "seq"),
    )
    out_specs = P("phase", "seq", None)
    return jax.shard_map(body, mesh=mesh, in_specs=in_specs, out_specs=out_specs, check_vma=False)
```

```python
import functools
import math

import jax
import jax.numpy as jnp
from jax import lax
from jax.experimental import pallas as pl
from jax.experimental.pallas import tpu as pltpu
from jax.sharding import PartitionSpec as P

HEADS = 16
KERNEL = 31
MESH = pl.DeviceIdType.MESH


def padded_2(block, sides, width):
    for axis, dim in sides:
        count = lax.axis_size(axis)
        forward = [(i, i + 1) for i in range(count - 1)]
        backward = [(target, source) for source, target in forward]
        low = lax.ppermute(
            lax.slice_in_dim(block, block.shape[dim] - width, None, axis=dim), axis, forward
        )
        high = lax.ppermute(lax.slice_in_dim(block, 0, width, axis=dim), axis, backward)
        block = jnp.concatenate([low, block, high], axis=dim)
    return block


def passed_along(block, axis, distance):
    devices = range(lax.axis_size(axis))
    route = [((i - distance) % len(devices), i) for i in devices]
    return lax.ppermute(block, axis, route)


def layer_norm(values):
    centre = values - jnp.mean(values, axis=-1, keepdims=True)
    spread = jnp.mean(centre * centre, axis=-1, keepdims=True)
    return centre * lax.rsqrt(spread + 1e-05)


def segment_ids(positions, lengths):
    order = jnp.arange(lengths.shape[0], dtype=jnp.int32)
    bounds = jnp.sum(jnp.where(order[None, :] <= order[:, None], lengths[None, :], 0), axis=1)
    return jnp.sum((positions[:, None] >= bounds[None, :]).astype(jnp.int32), axis=1)


def ring_index(place, shards):
    place = lax.rem(place + shards, shards)
    late = lax.div(place, shards // 2)
    return (1 - late) * (2 * place) + late * (2 * (shards - 1 - place) + 1)


def segment_of(positions, bounds):
    segment = jnp.zeros(positions.shape, jnp.int32)
    for bound in bounds:
        segment = segment + (positions >= bound).astype(jnp.int32)
    return segment


def block_kernel(
    shards,
    head_size,
    lengths_ref,
    frames_ref,
    taps_ref,
    query_ref,
    key_ref,
    value_ref,
    w_a_ref,
    w_b_ref,
    w_c_ref,
    handed_ref,
    hidden,
    qkv,
    full_a_ref,
    half_b_ref,
    full_c_ref,
    attended_ref,
    after,
    conv_rows,
    near,
    taps,
    padded,
    depthwise,
    deep_out,
    deep_in,
    leaving,
    query,
    keys,
    values,
    outbox,
    send_sem,
    recv_sem,
    own_sem,
    out_send,
    out_recv,
    in_sem,
    w_send,
    w_recv,
    rows_send,
    rows_recv,
    edge_send,
    edge_recv,
    deep_send,
    deep_recv,
    leave_send,
    leave_recv,
):
    rows = frames_ref.shape[0]
    depth = frames_ref.shape[1]
    width = query_ref.shape[1]
    part = w_b_ref.shape[1]
    me = lax.axis_index("seq")
    own_rows = pl.ds(pl.multiple_of(me * rows, rows), rows)
    loads_in = [pltpu.make_async_copy(frames_ref, hidden.at[own_rows, :], in_sem.at[3])]
    for i, ref in enumerate((query_ref, key_ref, value_ref)):
        loads_in.append(
            pltpu.make_async_copy(ref, qkv.at[:, pl.ds(i * width, width)], in_sem.at[i])
        )
    for copy in loads_in:
        copy.start()
    steps = shards // 2
    odd = lax.rem(me, 2)
    place = (1 - odd) * lax.div(me, 2) + odd * (shards - 1 - lax.div(me, 2))
    right, left = ring_index(place + 1, shards), ring_index(place - 1, shards)
    half = lax.rem(lax.div(me, 2), 2)
    upper = lax.div(me, 4)

    def partner_of(owner):
        return owner + 2 - 4 * lax.rem(lax.div(owner, 2), 2)

    def inner_of(owner):
        return lax.rem(lax.div(lax.div(owner, 2) + 1, 2), 2)

    beside = me + 1 - 2 * odd
    facing = me + 2 - 4 * upper
    partner = partner_of(me)
    inner = inner_of(me) == 1
    outer = inner_of(me) == 0
    home = inner_of(me) * me + (1 - inner_of(me)) * partner

    barrier = pltpu.get_barrier_semaphore()
    for away in range(1, shards):
        peer = lax.rem(me + away, shards)
        pl.semaphore_signal(barrier, inc=1, device_id={"seq": peer}, device_id_type=MESH)
    phase = lax.axis_index("phase")
    phases = lax.axis_size("phase")
    phase_next = lax.rem(phase + 1, phases)
    phase_back = lax.rem(phase + phases - 1, phases)
    for other in (phase_next, phase_back):
        for peer in (me, partner):
            pl.semaphore_signal(
                barrier, inc=1, device_id={"phase": other, "seq": peer}, device_id_type=MESH
            )

    loads_in[0].wait()
    pl.semaphore_wait(barrier, shards + 3)

    def remote(source, target, sent, got, peer, onward=None):
        place_of = {"seq": peer} if onward is None else {"phase": onward, "seq": peer}
        return pltpu.make_async_remote_copy(
            src_ref=source,
            dst_ref=target,
            send_sem=sent,
            recv_sem=got,
            device_id=place_of,
            device_id_type=MESH,
        )

    def hop(step, way, piece):
        owner = ring_index(place - step if way == 0 else place + step, shards)
        size = rows // 2
        block = hidden.at[pl.ds(pl.multiple_of(owner * rows + piece * size, 16), size), :]
        at = step * 2 + way
        peer = right if way == 0 else left
        return remote(block, block, send_sem.at[at, piece], recv_sem.at[at, piece], peer)

    def hops(step):
        pairs = [(way, piece) for piece in range(2) for way in range(2)]
        return [(way, piece) for way, piece in pairs if step < steps - 1 or way == piece]

    def forward(step):
        onward = hops(step + 1) if step < steps - 1 else ()
        for way, piece in hops(step):
            hop(step, way, piece).wait_recv()
            if (way, piece) in onward:
                hop(step + 1, way, piece).start()

    def project(owner):
        at = pl.ds(pl.multiple_of(owner * rows, rows), rows)
        block = layer_norm(hidden[at, :].astype(jnp.float32)).astype(jnp.bfloat16)
        both = jnp.dot(block, qkv[...], preferred_element_type=jnp.float32).astype(jnp.bfloat16)
        query[at, :] = both[:, :width] * jnp.bfloat16(1.0 / math.sqrt(head_size))
        keys[at, :] = both[:, width : 2 * width]
        values[at, :] = both[:, 2 * width :]

    fulls = ((w_a_ref, full_a_ref), (w_c_ref, full_c_ref), (w_b_ref, half_b_ref))
    wholes = range(2)

    def chunk(load, owner, first, size):
        full = fulls[load][1]
        if load == 2:
            return full.at[lax.div(owner, 2), pl.ds(first, size), :]
        cols = pl.ds(pl.multiple_of(lax.rem(owner, 2) * width, 128), width)
        return full.at[lax.div(owner, 2), pl.ds(first, size), cols]

    def w_copy(load, kind, piece):
        own = fulls[load][0]
        size = depth // 2
        owner = (me, me, me, partner, beside, facing, partner_of(facing), me)[kind]
        peer = (partner, beside, facing, facing, partner, beside, beside, beside)[kind]
        target = chunk(load, owner, piece * size, size)
        source = own.at[pl.ds(piece * size, size), :] if kind in (0, 1, 2, 7) else target
        return remote(
            source, target, w_send.at[load, kind, piece], w_recv.at[load, kind, piece], peer
        )

    def w_start(load, kind):
        for piece in wholes:
            w_copy(load, kind, piece).start()

    def w_wait(load, kind, then=()):
        for piece in wholes:
            w_copy(load, kind, piece).wait_recv()
            for more in then:
                w_copy(load, more, piece).start()

    for way, piece in hops(0):
        hop(0, way, piece).start()

    @pl.when(inner)
    def _():
        w_start(0, 1)
        w_start(1, 1)

    kept = [
        pltpu.make_async_copy(fulls[load][0], chunk(load, me, 0, depth), own_sem.at[load])
        for load in range(3)
    ]
    for copy in kept:
        copy.start()
    bounds = [lengths_ref[0]]
    for utt in range(1, lengths_ref.shape[0]):
        bounds.append(bounds[-1] + lengths_ref[utt])
    seg_col = segment_of(lax.broadcasted_iota(jnp.int32, (1, rows * shards), 1), bounds)
    margin = 16
    span = rows * steps
    first_row = upper * span
    for shift in range(near.shape[0]):
        positions = lax.broadcasted_iota(jnp.int32, near.shape[1:], 0)
        positions = positions + (first_row + shift - KERNEL // 2)
        near[shift] = jnp.where(positions >= 0, segment_of(positions, bounds), -1)
    outside = pl.multiple_of(upper * (span + margin), 16)
    conv_rows[pl.ds(outside, margin), :] = jnp.zeros((margin, depth), jnp.bfloat16)
    taps[...] = taps_ref[...].astype(jnp.float32)

    for copy in loads_in[1:]:
        copy.wait()
    project(me)
    for step in range(steps):
        forward(step)
        if step == steps - 2:

            @pl.when(outer)
            def _():
                w_start(0, 0)
                w_start(0, 7)

            @pl.when(inner)
            def _():
                w_start(0, 2)

        project(ring_index(place - 1 - step, shards))
        if step < steps - 1:
            project(ring_index(place + 1 + step, shards))

    lane = lax.broadcasted_iota(jnp.int32, (rows, width), 1)
    my_columns = pl.ds(pl.multiple_of(me * width, 128), width)

    def attend(owner):
        at = pl.ds(pl.multiple_of(owner * rows, rows), rows)
        block = query[at, :]
        positions = lax.broadcasted_iota(jnp.int32, (rows, 1), 0) + owner * rows
        allowed = segment_of(positions, bounds) == seg_col
        result = jnp.zeros((rows, width), jnp.float32)
        for head in range(width // head_size):
            mine = (lane >= head * head_size) & (lane < (head + 1) * head_size)
            scores = lax.dot_general(
                jnp.where(mine, block, jnp.bfloat16(0)),
                keys[...],
                (((1,), (1,)), ((), ())),
                preferred_element_type=jnp.float32,
            )
            scores = jnp.where(allowed, scores, -1e30)
            peak = jnp.max(scores, axis=1, keepdims=True)
            expw = jnp.exp(scores - peak)
            total = jnp.sum(expw, axis=1, keepdims=True)
            mixed = jnp.dot(
                expw.astype(jnp.bfloat16), values[...], preferred_element_type=jnp.float32
            )
            result = jnp.where(mine, mixed / total, result)
        return result.astype(jnp.bfloat16)

    def out_copy(turn, target):
        return remote(
            outbox.at[turn],
            attended_ref.at[:, my_columns],
            out_send.at[turn],
            out_recv.at[me],
            target,
        )

    turns = steps

    def target_of(turn):
        return 2 + lax.rem(home - 2 + 1 + turn, turns)

    for turn in range(turns):
        target = target_of(turn)
        outbox[turn, :rows, :] = attend(target)
        outbox[turn, rows:, :] = attend(partner_of(target))
        if turn < turns - 1:
            out_copy(turn, target).start()
        else:

            @pl.when(outer)
            def _():
                out_copy(turns - 1, partner).start()

            @pl.when(inner)
            def _():
                attended_ref[:, my_columns] = outbox[turns - 1]

        if turn == 2:

            @pl.when(inner)
            def _():
                w_wait(0, 0, (3,))
                w_wait(0, 2, (5,))

    @pl.when(outer)
    def _():
        w_wait(0, 7, (4,))
        w_start(2, 0)
        for piece in wholes:
            w_copy(2, 0, piece).wait_send()
        w_start(1, 0)
        w_start(1, 7)
        w_wait(1, 7, (4,))

    @pl.when(inner)
    def _():
        w_start(2, 2)

    slot_rows = [
        pl.multiple_of((owner - 4 * upper) * rows, 16) for owner in (me, partner)
    ]
    other_rows = [
        pl.multiple_of((owner - 4 * upper) * rows, 16)
        for owner in (beside, partner_of(beside))
    ]

    def rows_copy(slot):
        block = conv_rows.at[pl.ds(pl.multiple_of(slot_rows[slot] + margin, 16), rows), :]
        return remote(block, block, rows_send.at[slot], rows_recv.at[slot], beside)

    def edge_copy(turn):
        source = pl.multiple_of((1 - upper) * span + upper * margin, 16)
        target = pl.multiple_of(upper * (span + margin), 16)
        return remote(
            conv_rows.at[pl.ds(source, margin), :],
            conv_rows.at[pl.ds(target, margin), :],
            edge_send.at[turn],
            edge_recv,
            facing if turn == 0 else facing + 1 - 2 * odd,
        )

    lends = inner & (odd + upper == 1)
    reach = KERNEL // 2

    def gate(piece):
        for at in range(0, span + 2 * margin, (span + 2 * margin) // 2):
            block = slice(at, at + (span + 2 * margin) // 2)
            value = jnp.dot(
                conv_rows[block, :], half_b_ref[piece], preferred_element_type=jnp.float32
            )
            gates = jnp.dot(
                conv_rows[block, :], half_b_ref[2 + piece], preferred_element_type=jnp.float32
            )
            glu = (value * jax.nn.sigmoid(gates)).astype(jnp.bfloat16)
            padded[block, :] = glu.astype(jnp.float32)

    def columns_of(piece, side, at):
        return pl.ds(pl.multiple_of(piece * (2 * part) + side * part + at, 128), 128)

    def taps_of(piece, at):
        cols = columns_of(piece, odd, at)
        block = taps[:, cols]
        size = rows // 2
        for first in range(0, span, size):
            own = near[reach % 8, first + reach // 8 * 8 : first + reach // 8 * 8 + size, :]
            summed = jnp.zeros((size, 128), jnp.float32)
            for shift in range(8):
                start = first + margin - reach + shift
                ahead = padded[start : start + size + 24, at : at + 128]
                for skip in range(0, 32, 8):
                    offset = skip + shift
                    if offset < KERNEL:
                        term = ahead[skip : skip + size] * block[offset : offset + 1]
                        keep = near[shift, first + skip : first + skip + size, :] == own
                        summed = summed + jnp.where(keep, term, 0.0)
            depthwise[first : first + size, cols] = summed

    def deep_copy(order, at):
        turn = order * 2 + at // 128
        return remote(
            deep_out.at[turn], deep_in.at[turn], deep_send.at[turn], deep_recv.at[turn], beside
        )

    def piece_of(order):
        return upper if order == 0 else 1 - upper

    def convolve(order):
        piece = piece_of(order)
        gate(piece)
        for at in range(0, part, 128):
            taps_of(piece, at)
            cols = columns_of(piece, odd, at)
            for slot in range(2):
                deep_out[order * 2 + at // 128, slot * rows : (slot + 1) * rows, :] = depthwise[
                    pl.ds(other_rows[slot], rows), cols
                ].astype(jnp.bfloat16)
            deep_copy(order, at).start()

    def leave(turn, slot, owner):
        cols = pl.ds(pl.multiple_of(lax.div(owner, 2) * (2 * width), 128), 2 * width)
        return remote(
            leaving.at[pl.ds(slot * rows, rows), cols],
            handed_ref.at[:, cols],
            leave_send.at[turn, slot],
            leave_recv.at[turn],
            me if slot == 0 else partner,
            phase_next,
        )

    ends = (me, partner, facing, partner_of(facing))

    @pl.when(inner)
    def _():
        w_wait(0, 3, (6,))
        for away in range(1, shards):
            source = lax.rem(me + away, shards)
            remote(
                outbox.at[0],
                attended_ref.at[:, my_columns],
                out_send.at[0],
                out_recv.at[source],
                source,
            ).wait_recv()
        kept[0].wait()

        def output_part(owner):
            at = lax.div(owner, 2)
            cols = pl.ds(pl.multiple_of(at * (2 * width), 128), 2 * width)
            mixed = jnp.dot(attended_ref[...], full_a_ref[at], preferred_element_type=jnp.float32)
            for slot, source in enumerate((me, partner)):
                block = slice(slot * rows, (slot + 1) * rows)
                first = pl.ds(pl.multiple_of(source * rows, rows), rows)
                after[block, cols] = hidden[first, cols].astype(jnp.float32) + mixed[block]

        w_wait(0, 1)
        output_part(me)
        w_wait(0, 4)
        output_part(partner)
        w_wait(0, 5)
        output_part(facing)
        w_wait(0, 6)
        output_part(partner_of(facing))
        for slot in (0, 1):
            block = layer_norm(after[slot * rows : (slot + 1) * rows, :]).astype(jnp.bfloat16)
            at = pl.ds(pl.multiple_of(slot_rows[slot] + margin, 16), rows)
            conv_rows[at, :] = block
            if slot == 0:

                @pl.when(lends)
                def _():
                    for turn in range(2):
                        edge_copy(turn).start()

            rows_copy(slot).start()
        w_wait(2, 0, (3,))
        kept[2].wait()
        w_wait(2, 2)
        edge_copy(0).wait_recv()
        for slot in range(2):
            rows_copy(slot).wait_recv()
        w_start(1, 2)
        w_wait(1, 0, (3,))
        convolve(0)
        w_wait(1, 2, (5,))
        w_wait(2, 3)
        convolve(1)
        w_wait(1, 3, (6,))
        for order in range(2):
            for at in range(0, part, 128):
                deep_copy(order, at).wait_recv()
                cols = columns_of(piece_of(order), 1 - odd, at)
                for slot in range(2):
                    depthwise[pl.ds(slot_rows[slot], rows), cols] = deep_in[
                        order * 2 + at // 128, slot * rows : (slot + 1) * rows, :
                    ].astype(jnp.float32)
        kept[1].wait()
        for slot in (1, 0):
            block = layer_norm(depthwise[pl.ds(slot_rows[slot], rows), :])
            act = (block * jax.nn.sigmoid(block)).astype(jnp.bfloat16)
            at_rows = slice(slot * rows, (slot + 1) * rows)
            for turn, owner in enumerate(ends):
                if slot == 1:
                    w_wait(1, (1, 4, 5, 6)[turn])
                at = lax.div(owner, 2)
                cols = pl.ds(pl.multiple_of(at * (2 * width), 128), 2 * width)
                leaving[at_rows, cols] = (
                    after[at_rows, cols]
                    + jnp.dot(act, full_c_ref[at], preferred_element_type=jnp.float32)
                ).astype(jnp.bfloat16)
                leave(turn, slot, owner).start()

    for step in range(steps):
        for way, piece in hops(step):
            hop(step, way, piece).wait_send()
    for turn in range(turns - 1):
        out_copy(turn, target_of(turn)).wait_send()

    @pl.when(outer)
    def _():
        for copy in kept:
            copy.wait()
        out_copy(turns - 1, partner).wait_send()
        for load, kinds in ((0, (0, 4, 7)), (1, (0, 4, 7))):
            for kind in kinds:
                for piece in wholes:
                    w_copy(load, kind, piece).wait_send()

    @pl.when(inner)
    def _():
        for load, kinds in ((0, (1, 2, 3, 5, 6)), (1, (1, 2, 3, 5, 6)), (2, (2, 3))):
            for kind in kinds:
                for piece in wholes:
                    w_copy(load, kind, piece).wait_send()
        for slot in range(2):
            rows_copy(slot).wait_send()
        for order in range(2):
            for at in range(0, part, 128):
                deep_copy(order, at).wait_send()
        for turn, owner in enumerate(ends):
            for slot in range(2):
                leave(turn, slot, owner).wait_send()

    @pl.when(lends)
    def _():
        for turn in range(2):
            edge_copy(turn).wait_send()

    for turn, owner in enumerate(ends):
        leave(turn, 0, owner).wait_recv()


def block_call(shards, hidden, lengths, taps, weights):
    rows, depth = hidden.shape
    width = weights[0].shape[1]
    part = weights[4].shape[1]
    total = rows * shards
    steps = shards // 2
    margin = 16
    vmem = pl.BlockSpec(memory_space=pltpu.VMEM)
    smem = pl.BlockSpec(memory_space=pltpu.SMEM)
    anywhere = pl.BlockSpec(memory_space=pl.ANY)
    dma = pltpu.SemaphoreType.DMA
    bf16, f32 = jnp.bfloat16, jnp.float32
    return pl.pallas_call(
        functools.partial(block_kernel, shards, depth // HEADS),
        out_shape=jax.ShapeDtypeStruct((rows, depth), bf16),
        in_specs=[smem, anywhere, vmem] + [anywhere] * 6,
        out_specs=vmem,
        scratch_shapes=[
            pltpu.VMEM((total, depth), bf16),
            pltpu.VMEM((depth, 3 * width), bf16),
            pltpu.VMEM((shards // 2, depth, 2 * width), bf16),
            pltpu.VMEM((shards // 2, depth, part), bf16),
            pltpu.VMEM((shards // 2, depth, 2 * width), bf16),
            pltpu.VMEM((2 * rows, depth), bf16),
            pltpu.VMEM((2 * rows, depth), f32),
            pltpu.VMEM((total // 2 + 2 * margin, depth), bf16),
            pltpu.VMEM((8, total // 2 + 24, 128), jnp.int32),
            pltpu.VMEM(taps.shape, f32),
            pltpu.VMEM((total // 2 + 2 * margin, part), f32),
            pltpu.VMEM((total // 2, depth), f32),
            pltpu.VMEM((4, 2 * rows, 128), bf16),
            pltpu.VMEM((4, 2 * rows, 128), bf16),
            pltpu.VMEM((2 * rows, depth), bf16),
            pltpu.VMEM((total, width), bf16),
            pltpu.VMEM((total, width), bf16),
            pltpu.VMEM((total, width), bf16),
            pltpu.VMEM((steps, 2 * rows, width), bf16),
            dma((2 * steps, 2)),
            dma((2 * steps, 2)),
            dma((3,)),
            dma((steps,)),
            dma((shards,)),
            dma((4,)),
            dma((3, 8, 2)),
            dma((3, 8, 2)),
            dma((2,)),
            dma((2,)),
            dma((2,)),
            dma,
            dma((4,)),
            dma((4,)),
            dma((steps, 2)),
            dma((steps,)),
        ],
        compiler_params=pltpu.CompilerParams(
            collective_id=0, has_side_effects=True, vmem_limit_bytes=56 * 1024 * 1024
        ),
    )(lengths, hidden, taps, *weights)


def attention_general(hidden, utt_lengths, w_query, w_key, w_value, w_output, conv_in, conv_out):
    shards = lax.axis_size("seq")
    my_index = lax.axis_index("seq")
    local_rows = hidden.shape[0]
    width = hidden.shape[1]
    total_rows = local_rows * shards
    head_size = width // HEADS
    scale = 1.0 / math.sqrt(head_size)
    groups = min(HEADS, shards)
    group_heads = HEADS // groups
    parts = shards // groups
    part_rows = local_rows // parts
    group_width = group_heads * head_size
    full_query, full_key, full_value, full_output, full_conv_in, full_conv_out = (
        lax.all_gather(w_query, "seq", axis=1, tiled=True),
        lax.all_gather(w_key, "seq", axis=1, tiled=True),
        lax.all_gather(w_value, "seq", axis=1, tiled=True),
        lax.all_gather(w_output, "seq", axis=1, tiled=True),
        lax.all_gather(conv_in, "seq", axis=1, tiled=True),
        lax.all_gather(conv_out, "seq", axis=1, tiled=True),
    )
    normed = layer_norm(hidden.astype(jnp.float32)).astype(jnp.bfloat16)
    query = jnp.dot(normed, full_query, preferred_element_type=jnp.float32).astype(jnp.bfloat16)
    key_proj = jnp.dot(normed, full_key, preferred_element_type=jnp.float32).astype(jnp.bfloat16)
    value_proj = jnp.dot(normed, full_value, preferred_element_type=jnp.float32).astype(
        jnp.bfloat16
    )
    shaped = query.reshape(parts, part_rows, groups, group_width).transpose(2, 0, 1, 3)
    query_pieces = shaped.reshape(shards, part_rows, group_width)
    kv_local = jnp.concatenate(
        [
            key_proj.reshape(local_rows, groups, group_width),
            value_proj.reshape(local_rows, groups, group_width),
        ],
        axis=2,
    )
    copies = jnp.broadcast_to(
        kv_local.transpose(1, 0, 2)[:, None], (groups, parts, local_rows, 2 * group_width)
    )
    copies = copies.reshape(shards, local_rows, 2 * group_width)
    query_got, kv_got = (
        lax.all_to_all(query_pieces, "seq", split_axis=0, concat_axis=0, tiled=True),
        lax.all_to_all(copies, "seq", split_axis=0, concat_axis=0, tiled=True),
    )
    key_value = kv_got.reshape(total_rows, 2 * group_width)
    count = shards * part_rows
    my_part = my_index % parts
    row_ids = jnp.arange(count, dtype=jnp.int32)
    query_pos = row_ids // part_rows * local_rows + my_part * part_rows + row_ids % part_rows
    queries = query_got.reshape(count, group_heads, head_size)
    key_rows = key_value[:, :group_width].reshape(total_rows, group_heads, head_size)
    value_rows = key_value[:, group_width:].reshape(total_rows, group_heads, head_size)
    seg_all = segment_ids(jnp.arange(total_rows, dtype=jnp.int32), utt_lengths)
    seg_query = segment_ids(query_pos, utt_lengths)
    query_block = math.gcd(512, count)
    blocks = count // query_block

    def attend_block(operands):
        block_query, block_seg = operands
        scores = (
            jnp.einsum("qhd,khd->hqk", block_query, key_rows, preferred_element_type=jnp.float32)
            * scale
        )
        allowed = (block_seg[:, None] == seg_all[None, :])[None]
        scores = jnp.where(allowed, scores, -1e30)
        peak = jnp.max(scores, axis=2, keepdims=True)
        expw = jnp.where(allowed, jnp.exp(scores - peak), 0.0)
        total_weight = jnp.sum(expw, axis=2)
        mixed = jnp.einsum(
            "hqk,khd->hqd",
            expw.astype(jnp.bfloat16),
            value_rows,
            preferred_element_type=jnp.float32,
        )
        mixed = mixed / total_weight[:, :, None]
        return mixed.transpose(1, 0, 2).astype(jnp.bfloat16)

    attended = lax.map(
        attend_block,
        (
            queries.reshape(blocks, query_block, group_heads, head_size),
            seg_query.reshape(blocks, query_block),
        ),
    )
    outgoing = attended.reshape(shards, part_rows, group_width)
    returned = lax.all_to_all(outgoing, "seq", split_axis=0, concat_axis=0, tiled=True)
    attended_local = (
        returned.reshape(groups, parts, part_rows, group_width)
        .transpose(1, 2, 0, 3)
        .reshape(local_rows, width)
    )
    return attended_local, full_output, full_conv_in, full_conv_out


def body(frames, lengths, w_query, w_key, w_value, w_output, conv_in, conv_taps, conv_out):
    hidden = frames[0]
    utt_lengths = lengths[0]
    shards = lax.axis_size("seq")
    my_index = lax.axis_index("seq")
    local_rows = hidden.shape[0]
    width = hidden.shape[1]
    total_rows = local_rows * shards
    phases = lax.axis_size("phase")
    if phases > 2 and shards == 8 and width // shards == 128 and local_rows % 32 == 0:
        weights = (w_query[0], w_key[0], w_value[0], w_output[0], conv_in[0], conv_out[0])
        return block_call(shards, hidden, utt_lengths, conv_taps[0], weights)[None]
    attended_local, full_output, full_conv_in, full_conv_out = attention_general(
        hidden, utt_lengths, w_query[0], w_key[0], w_value[0], w_output[0], conv_in[0], conv_out[0]
    )
    after_attn = hidden.astype(jnp.float32) + jnp.dot(
        attended_local, full_output, preferred_element_type=jnp.float32
    )
    conv_normed = layer_norm(after_attn).astype(jnp.bfloat16)
    gates = jnp.dot(conv_normed, full_conv_in, preferred_element_type=jnp.float32)
    glu = (gates[:, :width] * jax.nn.sigmoid(gates[:, width:])).astype(jnp.bfloat16)
    reach = KERNEL // 2
    padded = padded_2(glu, (("seq", 0),), KERNEL // 2)
    padded_pos = my_index * local_rows - reach + jnp.arange(local_rows + 2 * reach, dtype=jnp.int32)
    inside = (padded_pos >= 0) & (padded_pos < total_rows)
    padded_seg = jnp.where(inside, segment_ids(padded_pos, utt_lengths), -1)
    own_seg = padded_seg[reach : reach + local_rows]
    taps = conv_taps[0]
    depthwise = jnp.zeros((local_rows, width), jnp.float32)
    for offset in range(KERNEL):
        keep = padded_seg[offset : offset + local_rows] == own_seg
        term = padded[offset : offset + local_rows].astype(jnp.float32) * taps[offset].astype(
            jnp.float32
        )
        depthwise = depthwise + jnp.where(keep[:, None], term, 0.0)
    conv_act = layer_norm(depthwise)
    conv_act = (conv_act * jax.nn.sigmoid(conv_act)).astype(jnp.bfloat16)
    block_out = (
        after_attn + jnp.dot(conv_act, full_conv_out, preferred_element_type=jnp.float32)
    ).astype(jnp.bfloat16)
    passed = passed_along(block_out, "phase", 1)
    return passed[None]


def solution(mesh):
    in_specs = (
        P("phase", "seq", None),
        P("phase", None),
        P("phase", None, "seq"),
        P("phase", None, "seq"),
        P("phase", None, "seq"),
        P("phase", None, "seq"),
        P("phase", None, "seq"),
        P("phase", None, None),
        P("phase", None, "seq"),
    )
    out_specs = P("phase", "seq", None)
    return jax.shard_map(body, mesh=mesh, in_specs=in_specs, out_specs=out_specs, check_vma=False)
```
